256 devices in a mesh: dp: 16 (over z, core), seq: 16 (over y, x).
Axes of the slice: x: 4, y: 4, z: 8, core: 2. Of those that a mesh axis runs over, the one named last changes fastest.
Arguments:
- queries: bfloat16 [16, 2048, 1024], P('dp', 'seq'), may hold values from -8 to 8
- key_vectors: bfloat16 [16, 2048, 1024], P('dp', 'seq'), may hold values from -8 to 8
- value_vectors: bfloat16 [16, 2048, 1024], P('dp', 'seq'), may hold values from -6 to 6
- out_grad: bfloat16 [16, 2048, 1024], P('dp', 'seq'), may hold values from -6 to 6
- proj_weight: bfloat16 [1024, 1024], P(None, 'seq'), may hold values from -0.1875 to 0.1875
- cluster_order: int32 [16, 2048], P('dp'), may hold values from 0 to 2047, as said below
- block_cols: int32 [16, 32, 16], P('dp'), may hold values from 0 to 31, as said below
- block_count: int32 [16, 32], P('dp'), may hold values from 5 to 16, as said below
Outputs:
- layer_out: bfloat16 [16, 2048, 1024], P('dp', 'seq')
- query_grad: bfloat16 [16, 2048, 1024], P('dp', 'seq')
- key_grad: bfloat16 [16, 2048, 1024], P('dp', 'seq')
- value_grad: bfloat16 [16, 2048, 1024], P('dp', 'seq')
- weight_grad: float32 [1024, 1024], P(None, 'seq')
The draws below stay inside these ranges and needn't reach their ends.
Inputs may be any that keep to these rules, and one draw needn't show every extreme that they name: `cluster_order`: each graph's row is a permutation of the 2048 nodes. `block_cols`: the entries of one list are distinct and the list of row block r begins with r itself; entries at positions block_count or later are ignored. `block_count`: some row block of every graph has 16 live entries.
All inputs are finite; a program needn't handle non-finite values.
Results may differ from the reference program's by a relative error of at most 0.029.
Values may be sent and summed in bfloat16 or wider, within the bound.
A program may use at most 64 MiB of HBM per device.

```python
import jax
import jax.numpy as jnp
from jax import lax

HEADS = 16
HEAD = 64
D = 1024
NODES = 2048
NBLK = 32
MAXB = 16
GRAPHS = 16


def cluster_setup(key):
    graph_ids = jnp.arange(GRAPHS)
    node_order = jax.vmap(lambda graph_idx: jax.random.permutation(jax.random.fold_in(key, 1000 + graph_idx), NODES))(graph_ids)
    return node_order.astype(jnp.int32)


def draw_queries(key, part):
    key = jax.random.fold_in(key, 5)
    sample = jnp.clip(jax.random.normal(key, (GRAPHS, NODES, D), jnp.float32), -4.0, 4.0)
    return sample.astype(jnp.bfloat16)


def draw_key_vectors(key, part):
    key = jax.random.fold_in(key, 6)
    sample = jnp.clip(jax.random.normal(key, (GRAPHS, NODES, D), jnp.float32), -4.0, 4.0)
    return sample.astype(jnp.bfloat16)


def draw_cluster_order(key, part):
    node_order = cluster_setup(key)
    return node_order


def draw_block_cols(key, part):
    key = jax.random.fold_in(key, 7)
    row_id = jnp.arange(NBLK)[:, None]
    column_id = jnp.arange(NBLK)[None, :]
    jitter = jax.random.randint(key, (GRAPHS, NBLK, NBLK), 0, 2 * NBLK)
    ranking = (jitter + jnp.abs(column_id - row_id)) * NBLK + column_id
    ranking = jnp.where(column_id == row_id, -1, ranking)
    chosen = jnp.argsort(ranking, axis=-1, stable=True)[..., :MAXB]
    return chosen.astype(jnp.int32)


def draw_block_count(key, part):
    key = jax.random.fold_in(key, 11)
    first_part, second_part, third_part = jax.random.split(key, 3)
    first_draw = jax.random.randint(first_part, (GRAPHS, NBLK), MAXB // 2, MAXB + 1)
    second_draw = jax.random.randint(second_part, (GRAPHS, NBLK), MAXB // 2, MAXB + 1)
    live_count = jnp.minimum(1 + first_draw * second_draw // MAXB, MAXB)
    dense_row = jax.random.randint(third_part, (GRAPHS,), 0, NBLK)
    live_count = live_count.at[jnp.arange(GRAPHS), dense_row].set(MAXB)
    return live_count.astype(jnp.int32)


def block_levels(key, dims, cuts, low, high):
    def one(position, blocks):
        heights = jax.random.uniform(jax.random.fold_in(jax.random.fold_in(key, 6), position), (blocks,), jnp.float32, low / len(cuts), high / len(cuts))
        return jnp.repeat(jnp.exp(heights), dims[position] // blocks).reshape((-1,) + (1,) * (len(dims) - position - 1))

    level = one(*cuts[0])
    for cut in cuts[1:]:
        level = level * one(*cut)
    return level


def centred(own_key, shape, deviation, reach, cuts=(), kind=jnp.bfloat16):
    entries = deviation * jax.random.normal(own_key, shape, jnp.float32)
    if cuts:
        entries = entries * block_levels(own_key, shape, cuts, -0.22, 0.18)
    return jnp.clip(entries, -reach, reach).astype(kind)


def setup_inputs(seed: int = 0) -> dict:
    arg_keys = jax.random.split(jax.random.key(seed), 9)
    return {
        "queries": draw_queries(jax.random.fold_in(arg_keys[8], 71), 0),
        "key_vectors": draw_key_vectors(jax.random.fold_in(arg_keys[8], 71), 0),
        "value_vectors": centred(arg_keys[2], (GRAPHS, NODES, D), 1.0, 6.0, ((0, 16), (1, 16))),
        "out_grad": centred(arg_keys[3], (GRAPHS, NODES, D), 1.0, 6.0, ((0, 16), (1, 16))),
        "proj_weight": centred(arg_keys[4], (D, D), D ** -0.5, 0.1875, ((1, 16),)),
        "cluster_order": draw_cluster_order(jax.random.fold_in(arg_keys[8], 71), 0),
        "block_cols": draw_block_cols(jax.random.fold_in(arg_keys[8], 71), 0),
        "block_count": draw_block_count(jax.random.fold_in(arg_keys[8], 71), 0),
    }


def head_pass(query_rows, key_rows, value_rows, upstream_rows, col_blocks, block_counts, score_scale):
    block_total = col_blocks.shape[0]
    list_len = col_blocks.shape[1]
    block_len = query_rows.shape[0] // block_total
    head_size = query_rows.shape[1]
    row_blocks = min(8, block_total)
    groups = block_total // row_blocks
    query_tiles = query_rows.reshape(groups, row_blocks, block_len, head_size)
    upstream_tiles = upstream_rows.reshape(groups, row_blocks, block_len, head_size)
    key_blocks = key_rows.reshape(block_total, block_len, head_size)
    value_blocks = value_rows.reshape(block_total, block_len, head_size)
    group_cols_all = col_blocks.reshape(groups, row_blocks, list_len)
    group_count_all = block_counts.reshape(groups, row_blocks)

    def group_step(state, inputs):
        key_acc, value_acc = state
        query_tile, upstream_tile, group_cols, group_count = inputs
        key_tiles = key_blocks[group_cols].astype(jnp.float32)
        value_tiles = value_blocks[group_cols].astype(jnp.float32)
        query_f = query_tile.astype(jnp.float32)
        upstream_f = upstream_tile.astype(jnp.float32)
        score = jnp.einsum('rid,rmjd->rimj', query_f, key_tiles) * score_scale
        live_mask = (jnp.arange(list_len)[None, :] < group_count[:, None])[:, None, :, None]
        masked = jnp.where(live_mask, score, -jnp.inf)
        row_max = jnp.max(masked, axis=(2, 3), keepdims=True)
        exp_terms = jnp.exp(masked - row_max)
        denominator = jnp.sum(exp_terms, axis=(2, 3), keepdims=True)
        softmax = exp_terms / denominator
        softmax_half = softmax.astype(jnp.bfloat16)
        output_tile = jnp.einsum('rimj,rmjd->rid', softmax_half.astype(jnp.float32), value_tiles).astype(jnp.bfloat16)
        row_delta = jnp.sum(output_tile.astype(jnp.float32) * upstream_f, axis=-1)[:, :, None, None]
        grad_softmax = jnp.einsum('rid,rmjd->rimj', upstream_f, value_tiles)
        grad_score = (score_scale * softmax * (grad_softmax - row_delta)).astype(jnp.bfloat16)
        grad_score_f = grad_score.astype(jnp.float32)
        grad_query = jnp.einsum('rimj,rmjd->rid', grad_score_f, key_tiles).astype(jnp.bfloat16)
        key_terms = jnp.einsum('rimj,rid->rmjd', grad_score_f, query_f)
        value_terms = jnp.einsum('rimj,rid->rmjd', softmax_half.astype(jnp.float32), upstream_f)
        flat_cols = group_cols.reshape(-1)
        key_acc = key_acc.at[flat_cols].add(key_terms.reshape(-1, block_len, head_size))
        value_acc = value_acc.at[flat_cols].add(value_terms.reshape(-1, block_len, head_size))
        return (key_acc, value_acc), (output_tile, grad_query)

    start_state = (jnp.zeros((block_total, block_len, head_size), jnp.float32),
                   jnp.zeros((block_total, block_len, head_size), jnp.float32))
    (key_acc, value_acc), (outputs, grad_queries) = lax.scan(
        group_step, start_state, (query_tiles, upstream_tiles, group_cols_all, group_count_all))
    return (outputs.reshape(-1, head_size), grad_queries.reshape(-1, head_size),
            key_acc.reshape(-1, head_size).astype(jnp.bfloat16),
            value_acc.reshape(-1, head_size).astype(jnp.bfloat16))


def reference(queries, key_vectors, value_vectors, out_grad, proj_weight, cluster_order, block_cols, block_count):
    score_scale = HEAD ** -0.5

    def per_graph(weight_sum, inputs):
        query_g, key_g, value_g, grad_g, node_order, col_blocks, block_counts = inputs
        inverse = jnp.zeros((NODES,), jnp.int32).at[node_order].set(jnp.arange(NODES, dtype=jnp.int32))
        upstream = jnp.dot(grad_g, proj_weight.T, preferred_element_type=jnp.float32).astype(jnp.bfloat16)

        def to_head_rows(array):
            return array[node_order].reshape(NODES, HEADS, HEAD).transpose(1, 0, 2)

        def single_head(arrays):
            return head_pass(arrays[0], arrays[1], arrays[2], arrays[3], col_blocks, block_counts, score_scale)

        outputs, grad_q, grad_k, grad_v = lax.map(
            single_head, (to_head_rows(query_g), to_head_rows(key_g), to_head_rows(value_g), to_head_rows(upstream)))

        def from_heads(array):
            return array.transpose(1, 0, 2).reshape(NODES, D)[inverse]

        attn = from_heads(outputs)
        layer_g = jnp.dot(attn, proj_weight, preferred_element_type=jnp.float32).astype(jnp.bfloat16)
        grad_term = jnp.dot(attn.T, grad_g, preferred_element_type=jnp.float32)
        return weight_sum + grad_term, (layer_g, from_heads(grad_q), from_heads(grad_k), from_heads(grad_v))

    weight_grad, (layer_out, query_grad, key_grad, value_grad) = lax.scan(
        per_graph, jnp.zeros((D, D), jnp.float32),
        (queries, key_vectors, value_vectors, out_grad, cluster_order, block_cols, block_count))
    return layer_out, query_grad, key_grad, value_grad, weight_grad
```

```python
import functools
import jax
import jax.numpy as jnp
from jax import lax
from jax.experimental import pallas as pl
from jax.experimental.pallas import tpu as pltpu
from jax.sharding import PartitionSpec as P

BLK = 64
F32 = jnp.float32
BF16 = jnp.bfloat16


def attention_kernel(
    cols_ref, count_ref, qb_in, kv_in, order_ref, oq_out, dkv_out,
    qb_ref, kv_ref, kvt_ref, score_ref, gsm_ref, acc_ref, oq_ref,
):
    nodes = qb_in.shape[0]
    nblk = nodes // BLK
    listed = cols_ref.shape[1]
    pairs = nblk // 2
    chunks = listed // 4
    order_col = jnp.transpose(
        jnp.concatenate(
            [order_ref[...].astype(F32),
             jnp.zeros((128 - order_ref.shape[0], 128), F32)], axis=0)
    ).astype(jnp.int32)
    lane_node = lax.broadcasted_iota(jnp.int32, (128, nodes), 1)
    low = lax.broadcasted_iota(jnp.int32, (128, 128), 1) < BLK
    zero = jnp.zeros((128, 128), BF16)
    rows = jnp.concatenate([qb_in[...], kv_in[...]], axis=1)
    for i in range(nodes // 128):
        pick = (lane_node == order_col[:, i:i + 1]).astype(F32).astype(BF16)
        moved = jnp.dot(pick, rows, preferred_element_type=F32)
        qb = moved[:, :128]
        qb_ref[i * 128:(i + 1) * 128, :] = jnp.where(low, qb * 0.125, qb).astype(BF16)
        kv = moved[:, 128:].astype(BF16)
        kv_ref[2 * i] = kv[:BLK]
        kv_ref[2 * i + 1] = kv[BLK:]
        kvt = jnp.transpose(moved[:, 128:])
        swap = pltpu.roll(kvt, BLK, 1)
        kvt = kvt.astype(BF16)
        swap = swap.astype(BF16)
        kvt_ref[0, 2 * i] = jnp.where(low, kvt, zero)
        kvt_ref[1, 2 * i] = jnp.where(low, zero, swap)
        kvt_ref[0, 2 * i + 1] = jnp.where(low, swap, zero)
        kvt_ref[1, 2 * i + 1] = jnp.where(low, zero, kvt)
    acc_ref[...] = jnp.zeros_like(acc_ref)

    lane = lax.broadcasted_iota(jnp.int32, (1, 128), 1)
    low64 = lax.broadcasted_iota(jnp.int32, (BLK, 128), 1) < BLK
    zero64 = jnp.zeros((BLK, 128), BF16)

    def pair_step(i, carry):
        first = 2 * i
        second = first + 1
        qb1 = qb_ref[pl.ds(pl.multiple_of(i * 128, 128), BLK), :]
        qb2 = qb_ref[pl.ds(pl.multiple_of(i * 128 + BLK, BLK), BLK), :]
        weights = jnp.concatenate(
            [
                jnp.concatenate([jnp.where(low64, qb1, zero64), zero64], axis=1),
                jnp.concatenate([zero64, jnp.where(low64, qb2, zero64)], axis=1),
                jnp.concatenate([jnp.where(low64, zero64, qb1), zero64], axis=1),
                jnp.concatenate([zero64, jnp.where(low64, zero64, qb2)], axis=1),
            ],
            axis=0,
        )
        live = jnp.where(lane < BLK, count_ref[first], count_ref[second])
        peak = jnp.full((8, 128), -jnp.inf, F32)
        for c in range(chunks):
            lhs = jnp.concatenate(
                [
                    jnp.concatenate(
                        [kv_ref[cols_ref[first, m]], kv_ref[cols_ref[second, m]]], axis=1)
                    for m in range(4 * c, 4 * c + 4)
                ],
                axis=0,
            )
            both = lax.dot_general(
                lhs, weights, (((1,), (1,)), ((), ())), preferred_element_type=F32)
            for k in range(4):
                m = 4 * c + k
                part = jnp.where(m < live, both[k * BLK:(k + 1) * BLK, :128], -jnp.inf)
                score_ref[m * BLK:(m + 1) * BLK, :] = part
                peak = jnp.maximum(peak, jnp.max(part.reshape(8, 8, 128), axis=0))
            gsm_ref[c * 256:(c + 1) * 256, :] = both[:, 128:]
        peak = jnp.max(peak, axis=0, keepdims=True)
        total = jnp.zeros((8, 128), F32)
        delta = jnp.zeros((8, 128), F32)
        for c in range(chunks):
            rows = slice(c * 256, (c + 1) * 256)
            terms = jnp.exp(score_ref[rows, :] - peak)
            score_ref[rows, :] = terms
            total = total + jnp.sum(terms.reshape(32, 8, 128), axis=0)
            delta = delta + jnp.sum((terms * gsm_ref[rows, :]).reshape(32, 8, 128), axis=0)
        inv = 1.0 / jnp.sum(total, axis=0, keepdims=True)
        delta = jnp.sum(delta, axis=0, keepdims=True) * inv
        back = jnp.zeros((256, 256), F32)
        swapped = jnp.concatenate([weights[128:], weights[:128]], axis=0)
        for c in range(chunks):
            rows = slice(c * 256, (c + 1) * 256)
            soft = score_ref[rows, :] * inv
            grad = soft * (gsm_ref[rows, :] - delta)
            both = jnp.concatenate([soft.astype(BF16), grad.astype(BF16)], axis=1)
            key_terms = jnp.dot(both, swapped, preferred_element_type=F32)
            for k in range(4):
                m = 4 * c + k
                acc_ref[cols_ref[first, m]] += key_terms[k * BLK:(k + 1) * BLK, :128]
                acc_ref[cols_ref[second, m]] += key_terms[k * BLK:(k + 1) * BLK, 128:]
            sides = []
            for row in (first, second):
                sides.append(jnp.concatenate(
                    [
                        kvt_ref[0, cols_ref[row, m]] + kvt_ref[1, cols_ref[row, m + 1]]
                        for m in range(4 * c, 4 * c + 4, 2)
                    ],
                    axis=1,
                ))
            back = back + jnp.dot(
                jnp.concatenate(sides, axis=0), both, preferred_element_type=F32)
        outputs = jnp.where(low64, back[BLK:128, :128], back[128 + BLK:, :128])
        grad_q = jnp.where(low64, back[:BLK, 128:], back[128:128 + BLK, 128:]) * 0.125
        here = pl.ds(pl.multiple_of(i * 128, 128), 128)
        oq_ref[:BLK, here] = outputs.astype(BF16)
        oq_ref[BLK:, here] = grad_q.astype(BF16)
        return carry

    lax.fori_loop(0, pairs, pair_step, 0)

    order_row = jnp.concatenate([order_ref[i:i + 1, :] for i in range(nodes // 128)], axis=1)
    grad_kv = acc_ref[...].reshape(nodes, 128).astype(BF16)
    for j in range(nodes // 128):
        row_node = lax.broadcasted_iota(jnp.int32, (128, nodes), 0) + j * 128
        pick = (row_node == order_row).astype(F32).astype(BF16)
        oq_out[j] = lax.dot_general(
            pick, oq_ref[...], (((1,), (1,)), ((), ())), preferred_element_type=F32).astype(BF16)
        dkv_out[j] = jnp.dot(pick, grad_kv, preferred_element_type=F32).astype(BF16)


def attention(qb, kv, order, cols, count):
    nodes = qb.shape[0]
    nblk, listed = cols.shape
    smem = pl.BlockSpec(memory_space=pltpu.SMEM)
    vmem = pl.BlockSpec(memory_space=pltpu.VMEM)
    return pl.pallas_call(
        attention_kernel,
        out_shape=(jax.ShapeDtypeStruct((nodes // 128, 128, 128), BF16),) * 2,
        in_specs=[smem, smem, vmem, vmem, vmem],
        out_specs=(vmem, vmem),
        scratch_shapes=[
            pltpu.VMEM((nodes, 128), BF16),
            pltpu.VMEM((nblk, BLK, 128), BF16),
            pltpu.VMEM((2, nblk, 128, 128), BF16),
            pltpu.VMEM((listed * BLK, 128), F32),
            pltpu.VMEM((listed * BLK, 128), F32),
            pltpu.VMEM((nblk, BLK, 128), F32),
            pltpu.VMEM((128, nodes), BF16),
        ],
        compiler_params=pltpu.CompilerParams(vmem_limit_bytes=48 * 1024 * 1024),
        name="head_attention",
    )(cols, count, qb, kv, order.reshape(nodes // 128, 128))

MESH = pl.DeviceIdType.MESH
SIDE = 4


def greet(devices):
    barrier = pltpu.get_barrier_semaphore()
    for device in devices:
        pl.semaphore_signal(barrier, inc=1, device_id=device, device_id_type=MESH)
    pl.semaphore_wait(barrier, len(devices))


def push(src, dst, send_sem, recv_sem, device):
    copy = pltpu.make_async_remote_copy(
        src_ref=src, dst_ref=dst, send_sem=send_sem, recv_sem=recv_sem,
        device_id=device, device_id_type=MESH)
    copy.start()
    return copy


def beside(a, b):
    return jnp.concatenate([a, b], axis=1)


def inward_kernel(
    q_ref, k_ref, v_ref, g_ref, w_ref, qb_ref, kv_ref, wt_ref,
    up_ref, qb_out, kv_out,
    w1_send, w1_recv, w2_send, w2_recv, core_send, core_recv,
    kv_send, kv_recv, qb_send, qb_recv,
):
    dp, me = lax.axis_index("dp"), lax.axis_index("seq")
    seq = kv_ref.shape[0]
    y, x = me // SIDE, me % SIDE
    core = dp % 2
    mate = (dp + 1 - 2 * core, me)
    peers = [lax.rem(me + i, seq) for i in range(1, seq)]
    xs = [(y, lax.rem(x + i, SIDE)) for i in range(1, SIDE)]
    ys = [(lax.rem(y + i, SIDE), x) for i in range(1, SIDE)]
    x_peers = [(dp, y * SIDE + at) for _, at in xs]
    y_peers = [(dp, at * SIDE + x) for at, _ in ys]
    greet([(dp, p) for p in peers] + [mate])

    share = w_ref.shape[1]
    rows = share // 4
    eye = (lax.broadcasted_iota(jnp.int32, (share, share), 0)
           == lax.broadcasted_iota(jnp.int32, (share, share), 1)).astype(jnp.float32)
    wt_ref[y, x] = lax.dot_general(
        eye.astype(jnp.bfloat16), w_ref[...], (((1,), (1,)), ((), ())),
        preferred_element_type=jnp.float32).astype(jnp.bfloat16)
    start_a = pl.multiple_of(core * 2 * rows, 2 * rows)
    half_a = pl.ds(start_a, rows)
    half_b = pl.ds(pl.multiple_of(start_a + rows, rows), rows)
    first = []
    for i in range(SIDE - 1):
        for n, (part, targets) in enumerate(((half_a, x_peers), (half_b, y_peers))):
            piece = wt_ref.at[y, x, part]
            first.append(push(piece, piece, w1_send.at[n, i], w1_recv.at[n, i], targets[i]))

    width = 64
    for j in range(seq // 2):
        lanes = slice(2 * width * j, 2 * width * (j + 1))
        k, v = k_ref[:, lanes], v_ref[:, lanes]
        kv_out[2 * j] = beside(k[:, :width], v[:, :width])
        kv_out[2 * j + 1] = beside(k[:, width:], v[:, width:])
    kv_ref[me] = kv_out[me]
    kv_copies = [
        push(kv_out.at[p], kv_ref.at[me], kv_send.at[i], kv_recv.at[i], (dp, p))
        for i, p in enumerate(peers)]

    second, across = [], []
    for copy in first:
        copy.wait_recv()
    for i in range(SIDE - 1):
        for n, (part, sources) in enumerate(((half_a, xs), (half_b, ys))):
            piece = wt_ref.at[sources[i][0], sources[i][1], part]
            across.append(push(piece, piece, core_send.at[n, i], core_recv.at[n, i], mate))
    for i in range(SIDE - 1):
        piece = wt_ref.at[y, :, half_a]
        second.append(push(piece, piece, w2_send.at[0, i], w2_recv.at[0, i], y_peers[i]))
        piece = wt_ref.at[:, x, half_b]
        second.append(push(piece, piece, w2_send.at[1, i], w2_recv.at[1, i], x_peers[i]))
    for i in range(SIDE - 1):
        back = SIDE - 1 - i
        second[2 * i].wait_recv()
        piece = wt_ref.at[lax.rem(y + back, SIDE), :, half_a]
        across.append(push(piece, piece, core_send.at[2, i], core_recv.at[2, i], mate))
        second[2 * i + 1].wait_recv()
        piece = wt_ref.at[:, lax.rem(x + back, SIDE), half_b]
        across.append(push(piece, piece, core_send.at[3, i], core_recv.at[3, i], mate))
    for copy in across:
        copy.wait_recv()

    up_ref[...] = jnp.dot(
        g_ref[...], wt_ref[...].reshape(seq * share, wt_ref.shape[3]),
        preferred_element_type=jnp.float32).astype(jnp.bfloat16)
    for j in range(seq // 2):
        lanes = slice(2 * width * j, 2 * width * (j + 1))
        q, b = q_ref[:, lanes], up_ref[:, lanes]
        qb_out[2 * j] = beside(q[:, :width], b[:, :width])
        qb_out[2 * j + 1] = beside(q[:, width:], b[:, width:])
    qb_ref[me] = qb_out[me]
    qb_copies = [
        push(qb_out.at[p], qb_ref.at[me], qb_send.at[i], qb_recv.at[i], (dp, p))
        for i, p in enumerate(peers)]
    for copy in kv_copies + qb_copies:
        copy.wait_recv()
    for copy in first + second + across + kv_copies + qb_copies:
        copy.wait_send()


def inward(queries, keys, values, grads, weight, seq):
    nodes, depth = queries.shape
    share = weight.shape[1]
    vmem = pl.BlockSpec(memory_space=pltpu.VMEM)
    dma = pltpu.SemaphoreType.DMA
    bf16 = jnp.bfloat16
    side = SIDE - 1
    return pl.pallas_call(
        inward_kernel,
        out_shape=(
            jax.ShapeDtypeStruct((seq, nodes, 128), bf16),
            jax.ShapeDtypeStruct((seq, nodes, 128), bf16),
            jax.ShapeDtypeStruct((SIDE, SIDE, share, depth), bf16),
        ),
        in_specs=[vmem] * 5,
        out_specs=(vmem,) * 3,
        scratch_shapes=[
            pltpu.VMEM((nodes, depth), bf16),
            pltpu.VMEM((seq, nodes, 128), bf16),
            pltpu.VMEM((seq, nodes, 128), bf16),
            dma((2, side)), dma((2, side)), dma((2, side)), dma((2, side)),
            dma((4, side)), dma((4, side)),
            dma((seq - 1,)), dma((seq - 1,)), dma((seq - 1,)), dma((seq - 1,)),
        ],
        compiler_params=pltpu.CompilerParams(
            collective_id=0, has_side_effects=True, vmem_limit_bytes=48 * 1024 * 1024),
        name="inward",
    )(queries, keys, values, grads, weight)


def outward_kernel(
    oq_ref, kv_ref, g_ref, wt_ref,
    layer_ref, dq_ref, dk_ref, dv_ref, wg_ref,
    oq_in, kv_in, attn_ref, part_ref, mate_out, mate_in,
    sum_ref, half_ref, line_in, cross_out, cross_in, z_out, z_in, all_in,
    oq_send, oq_recv, kv_send, kv_recv, mate_send, mate_recv,
    line_send, line_recv, cross_send, cross_recv, z_send, z_recv, all_send, all_recv,
):
    dp, me = lax.axis_index("dp"), lax.axis_index("seq")
    seq = oq_ref.shape[0]
    dps = all_in.shape[0]
    nz = dps // 2
    f32, bf16 = jnp.float32, jnp.bfloat16
    y, x = me // SIDE, me % SIDE
    core, z = dp % 2, dp // 2
    mate = (dp + 1 - 2 * core, me)
    peers = [lax.rem(me + i, seq) for i in range(1, seq)]
    dp_peers = [lax.rem(dp + i, dps) for i in range(1, dps)]
    z_peers = [lax.rem(z + i, nz) for i in range(1, nz)]
    xs = [lax.rem(x + i, SIDE) for i in range(1, SIDE)]
    ys = [lax.rem(y + i, SIDE) for i in range(1, SIDE)]
    greet([(dp, p) for p in peers] + [(p, me) for p in dp_peers])

    oq_in[me] = oq_ref[me]
    oq_copies = [
        push(oq_ref.at[p], oq_in.at[me], oq_send.at[i], oq_recv.at[i], (dp, p))
        for i, p in enumerate(peers)]
    kv_in[me] = kv_ref[me]
    kv_copies = [
        push(kv_ref.at[p], kv_in.at[me], kv_send.at[i], kv_recv.at[i], (dp, p))
        for i, p in enumerate(peers)]

    width = 64
    for copy in oq_copies:
        copy.wait_recv()
    for j in range(seq // 2):
        lanes = slice(2 * width * j, 2 * width * (j + 1))
        a, b = oq_in[2 * j], oq_in[2 * j + 1]
        attn_ref[:, lanes] = beside(a[:, :width], b[:, :width])
        dq_ref[:, lanes] = beside(a[:, width:], b[:, width:])

    depth = attn_ref.shape[1]
    share = depth // seq
    keep = pl.ds(pl.multiple_of(core * (share // 2), share // 2), share // 2)
    give = pl.ds(pl.multiple_of((1 - core) * (share // 2), share // 2), share // 2)
    mate_copies = []
    for c in range(SIDE):
        part_ref[c] = lax.dot_general(
            g_ref[:, c * SIDE * share:(c + 1) * SIDE * share], attn_ref[...],
            (((0,), (0,)), ((), ())), preferred_element_type=f32).reshape(SIDE, share, depth)
        mate_out[c] = part_ref[c, :, give, :].astype(bf16)
        mate_copies.append(push(
            mate_out.at[c], mate_in.at[c], mate_send.at[c], mate_recv.at[c], mate))
    layer_ref[...] = lax.dot_general(
        attn_ref[...], wt_ref[...].reshape(depth, depth), (((1,), (1,)), ((), ())),
        preferred_element_type=f32).astype(bf16)
    for c in range(SIDE):
        mate_copies[c].wait_recv()
        total = part_ref[c, :, keep, :] + mate_in[c].astype(f32)
        sum_ref[c] = total
        half_ref[c] = total.astype(bf16)
    rows = share // 4
    line = []
    for i in range(SIDE - 1):
        line.append(push(
            half_ref.at[:, xs[i], :rows], line_in.at[0, i],
            line_send.at[0, i], line_recv.at[0, i], (dp, y * SIDE + xs[i])))
        line.append(push(
            half_ref.at[ys[i], :, rows:], line_in.at[1, i],
            line_send.at[1, i], line_recv.at[1, i], (dp, ys[i] * SIDE + x)))
    for copy in line:
        copy.wait_recv()
    sum_a = sum_ref[:, pl.ds(x, 1), :rows, :].reshape(SIDE, rows, depth)
    sum_b = sum_ref[pl.ds(y, 1), :, rows:, :].reshape(SIDE, rows, depth)
    for i in range(SIDE - 1):
        sum_a += line_in[0, i].astype(f32)
        sum_b += line_in[1, i].astype(f32)
    cross_out[0] = sum_a.astype(bf16)
    cross_out[1] = sum_b.astype(bf16)
    cross = []
    for i in range(SIDE - 1):
        cross.append(push(
            cross_out.at[0, ys[i]], cross_in.at[0, i],
            cross_send.at[0, i], cross_recv.at[0, i], (dp, ys[i] * SIDE + x)))
        cross.append(push(
            cross_out.at[1, xs[i]], cross_in.at[1, i],
            cross_send.at[1, i], cross_recv.at[1, i], (dp, y * SIDE + xs[i])))
    for copy in cross:
        copy.wait_recv()
    shard_a = cross_out[0, y].astype(f32)
    shard_b = cross_out[1, x].astype(f32)
    for i in range(SIDE - 1):
        shard_a += cross_in[0, i].astype(f32)
        shard_b += cross_in[1, i].astype(f32)
    shard = jnp.concatenate([shard_a, shard_b], axis=0)
    lanes = depth // nz
    for i in range(nz):
        z_out[i] = shard[:, i * lanes:(i + 1) * lanes].astype(bf16)
    z_copies = [
        push(z_out.at[p], z_in.at[i], z_send.at[i], z_recv.at[i], (2 * p + core, me))
        for i, p in enumerate(z_peers)]
    for copy in z_copies:
        copy.wait_recv()
    mine = z_out[z].astype(f32)
    for i in range(nz - 1):
        mine += z_in[i].astype(f32)
    all_in[dp] = mine.astype(bf16)
    all_copies = [
        push(all_in.at[dp], all_in.at[dp], all_send.at[i], all_recv.at[i], (p, me))
        for i, p in enumerate(dp_peers)]

    for copy in kv_copies:
        copy.wait_recv()
    for j in range(seq // 2):
        there = slice(2 * width * j, 2 * width * (j + 1))
        a, b = kv_in[2 * j], kv_in[2 * j + 1]
        dk_ref[:, there] = beside(a[:, :width], b[:, :width])
        dv_ref[:, there] = beside(a[:, width:], b[:, width:])
    for copy in all_copies:
        copy.wait_recv()
    for i in range(nz):
        tile = jnp.concatenate([all_in[2 * i], all_in[2 * i + 1]], axis=0).astype(f32)
        wg_ref[i * lanes:(i + 1) * lanes, :] = jnp.transpose(tile)
    for copy in oq_copies + kv_copies + mate_copies + line + cross + z_copies + all_copies:
        copy.wait_send()


def outward(oq, kv, grads, wt, dps):
    seq, nodes, _ = oq.shape
    depth = grads.shape[1]
    share = depth // seq
    nz = dps // 2
    rows = share // 4
    vmem = pl.BlockSpec(memory_space=pltpu.VMEM)
    dma = pltpu.SemaphoreType.DMA
    f32, bf16 = jnp.float32, jnp.bfloat16
    side = SIDE - 1
    flat = jax.ShapeDtypeStruct((nodes, depth), bf16)
    return pl.pallas_call(
        outward_kernel,
        out_shape=(flat, flat, flat, flat, jax.ShapeDtypeStruct((depth, share), f32)),
        in_specs=[vmem] * 4,
        out_specs=(vmem,) * 5,
        scratch_shapes=[
            pltpu.VMEM((seq, nodes, 128), bf16),
            pltpu.VMEM((seq, nodes, 128), bf16),
            pltpu.VMEM((nodes, depth), bf16),
            pltpu.VMEM((SIDE, SIDE, share, depth), f32),
            pltpu.VMEM((SIDE, SIDE, share // 2, depth), bf16),
            pltpu.VMEM((SIDE, SIDE, share // 2, depth), bf16),
            pltpu.VMEM((SIDE, SIDE, share // 2, depth), f32),
            pltpu.VMEM((SIDE, SIDE, share // 2, depth), bf16),
            pltpu.VMEM((2, side, SIDE, rows, depth), bf16),
            pltpu.VMEM((2, SIDE, rows, depth), bf16),
            pltpu.VMEM((2, side, rows, depth), bf16),
            pltpu.VMEM((nz, share // 2, depth // nz), bf16),
            pltpu.VMEM((max(nz - 1, 1), share // 2, depth // nz), bf16),
            pltpu.VMEM((dps, share // 2, depth // nz), bf16),
            dma((seq - 1,)), dma((seq - 1,)), dma((seq - 1,)), dma((seq - 1,)),
            dma((SIDE,)), dma((SIDE,)),
            dma((2, side)), dma((2, side)), dma((2, side)), dma((2, side)),
            dma((max(nz - 1, 1),)), dma((max(nz - 1, 1),)), dma((dps - 1,)), dma((dps - 1,)),
        ],
        compiler_params=pltpu.CompilerParams(
            collective_id=1, has_side_effects=True, vmem_limit_bytes=56 * 1024 * 1024),
        name="outward",
    )(oq, kv, grads, wt)


def on_device(queries, key_vectors, value_vectors, out_grad, proj_weight,
              cluster_order, block_cols, block_count):
    seq, dps = lax.axis_size("seq"), lax.axis_size("dp")
    qb, kv, wt = inward(
        queries[0], key_vectors[0], value_vectors[0], out_grad[0], proj_weight, seq)
    nodes = cluster_order.shape[1]
    oq, dkv = attention(
        qb.reshape(nodes, 128), kv.reshape(nodes, 128),
        cluster_order[0], block_cols[0], block_count[0])
    layer, dq, dk, dv, wg = outward(oq, dkv, out_grad[0], wt, dps)
    return layer[None], dq[None], dk[None], dv[None], wg


def solution(mesh):
    rows = P("dp", "seq", None)
    return jax.shard_map(
        on_device,
        mesh=mesh,
        in_specs=(rows, rows, rows, rows, P(None, "seq"),
                  P("dp", None), P("dp", None, None), P("dp", None)),
        out_specs=(rows, rows, rows, rows, P(None, "seq")),
        check_vma=False,
    )
```

```python
import jax
import jax.numpy as jnp
from jax import lax
from jax.experimental import pallas as pl
from jax.experimental.pallas import tpu as pltpu
from jax.sharding import PartitionSpec as P

MESH = pl.DeviceIdType.MESH
SIDE = 4
BLK = 64
F32 = jnp.float32
BF16 = jnp.bfloat16
TRANS_B = (((1,), (1,)), ((), ()))


def push(src, dst, sems, at, device):
    copy = pltpu.make_async_remote_copy(
        src_ref=src, dst_ref=dst, send_sem=sems[0].at[at], recv_sem=sems[1].at[at],
        device_id=device, device_id_type=MESH)
    copy.start()
    return copy


def beside(a, b):
    return jnp.concatenate([a, b], axis=1)


def above(*parts):
    return jnp.concatenate(parts, axis=0)


def fused_kernel(
    cols_ref, count_ref, cols_vec, count_vec, order_ref, q_hbm, k_hbm, v_hbm, g_hbm, w_hbm,
    layer_ref, dq_ref, dk_ref, dv_ref, wg_ref,
    q_ref, k_ref, v_ref, g_ref, wt_ref, up_ref, slots_vec, slots_ref,
    qk_out, v_out, b_out, x_ref, v_in, b_in,
    pick_ref, unpick_ref, qq_ref, kk_ref, vv_ref, bb_ref, kt_ref, vt_ref, bt_ref,
    score_ref, soft_ref, ot_ref, term_ref, grads_ref,
    o_out, dkv_out, dq_out, o_in, dkv_in, dq_in,
    attn_ref, part_ref, mate_out, mate_in, sum_ref, half_ref, line_in, cross_out, cross_in,
    z_out, z_in, all_in,
    in_sem, slot_sem, w1_sems, w2_sems, core_sems, qk_sems, v_sems, b_sems,
    o_sems, dkv_sems, dq_sems, mate_sems, line_sems, cross_sems, z_sems, all_sems,
):
    dp, me = lax.axis_index("dp"), lax.axis_index("seq")
    seq, half_nodes, _ = v_out.shape
    dps = all_in.shape[0]
    nz = dps // 2
    nodes_dev = 2 * half_nodes
    nodes = seq * nodes_dev
    nblk = nodes // BLK
    listed = cols_ref.shape[0]
    chunks = listed // 4
    quads = nblk // 4
    depth = q_ref.shape[1]
    share = depth // seq
    y, x = me // SIDE, me % SIDE
    core, z = dp % 2, dp // 2
    mate = (dp + 1 - 2 * core, me)
    peers = [lax.rem(me + i, seq) for i in range(1, seq)]
    dp_peers = [lax.rem(dp + i, dps) for i in range(1, dps)]
    z_peers = [lax.rem(z + i, nz) for i in range(1, nz)]
    xs = [lax.rem(x + i, SIDE) for i in range(1, SIDE)]
    ys = [lax.rem(y + i, SIDE) for i in range(1, SIDE)]
    x_peers = [(dp, y * SIDE + at) for at in xs]
    y_peers = [(dp, at * SIDE + x) for at in ys]
    low128 = lax.broadcasted_iota(jnp.int32, (128, 128), 1) < BLK
    low = lax.broadcasted_iota(jnp.int32, (BLK, 128), 1) < BLK
    zero = jnp.zeros((BLK, 128), BF16)
    zero128 = jnp.zeros((128, 128), BF16)

    loads = [
        pltpu.make_async_copy(src, dst, in_sem.at[i])
        for i, (src, dst) in enumerate((
            (w_hbm, wt_ref.at[y, x]), (k_hbm, k_ref), (q_hbm, q_ref), (v_hbm, v_ref),
            (g_hbm, g_ref)))]
    for load in loads:
        load.start()
    barrier = pltpu.get_barrier_semaphore()
    for device in [(dp, p) for p in peers] + [(p, me) for p in dp_peers]:
        pl.semaphore_signal(barrier, inc=1, device_id=device, device_id_type=MESH)
    pl.semaphore_wait(barrier, seq + dps - 2)

    rows = share // 4
    start_a = pl.multiple_of(core * 2 * rows, 2 * rows)
    half_a = pl.ds(start_a, rows)
    half_b = pl.ds(pl.multiple_of(start_a + rows, rows), rows)
    loads[0].wait()
    first, second, across = [], [], []
    for i in range(SIDE - 1):
        piece = wt_ref.at[y, x, half_a]
        first.append(push(piece, piece, w1_sems, (0, i), x_peers[i]))
        piece = wt_ref.at[y, x, half_b]
        first.append(push(piece, piece, w1_sems, (1, i), y_peers[i]))

    loads[1].wait()
    loads[2].wait()
    for j in range(seq // 2):
        lanes = slice(128 * j, 128 * (j + 1))
        q, k = q_ref[:, lanes], k_ref[:, lanes]
        qk_out[2 * j] = beside(q[:, :BLK], k[:, :BLK])
        qk_out[2 * j + 1] = beside(q[:, BLK:], k[:, BLK:])
    own = pl.ds(pl.multiple_of(me * nodes_dev, nodes_dev), nodes_dev)
    x_ref[own, :128] = qk_out[me]
    qk_copies = [
        push(qk_out.at[p], x_ref.at[own, pl.ds(0, 128)], qk_sems, i, (dp, p))
        for i, p in enumerate(peers)]

    def fold(ref, out):
        for j in range(seq // 2):
            tile = ref[:, 128 * j:128 * (j + 1)]
            out[2 * j] = beside(tile[:half_nodes, :BLK], tile[half_nodes:, :BLK])
            out[2 * j + 1] = beside(tile[:half_nodes, BLK:], tile[half_nodes:, BLK:])

    def unfold(ref, out):
        for j in range(seq // 2):
            lanes = slice(128 * j, 128 * (j + 1))
            a, b = ref[2 * j], ref[2 * j + 1]
            out[:half_nodes, lanes] = beside(a[:, :BLK], b[:, :BLK])
            out[half_nodes:, lanes] = beside(a[:, BLK:], b[:, BLK:])

    loads[3].wait()
    fold(v_ref, v_out)
    v_in[me] = v_out[me]
    v_copies = [
        push(v_out.at[p], v_in.at[me], v_sems, i, (dp, p)) for i, p in enumerate(peers)]

    order = order_ref[...]
    order_col = jnp.transpose(
        above(order.astype(F32), jnp.zeros((128 - order.shape[0], 128), F32))).astype(jnp.int32)
    lane_node = lax.broadcasted_iota(jnp.int32, (128, nodes), 1)
    for i in range(nodes // 128):
        pick_ref[128 * i:128 * (i + 1), :] = (
            lane_node == order_col[:, i:i + 1]).astype(F32).astype(BF16)

    for copy in first:
        copy.wait_recv()
    for i in range(SIDE - 1):
        piece = wt_ref.at[y, :, half_a]
        second.append(push(piece, piece, w2_sems, (0, i), y_peers[i]))
        piece = wt_ref.at[:, x, half_b]
        second.append(push(piece, piece, w2_sems, (1, i), x_peers[i]))
    for i in range(SIDE - 1):
        piece = wt_ref.at[y, xs[i], half_a]
        across.append(push(piece, piece, core_sems, (0, i), mate))
        piece = wt_ref.at[ys[i], x, half_b]
        across.append(push(piece, piece, core_sems, (1, i), mate))

    order_row = jnp.concatenate([order[i:i + 1, :] for i in range(nodes // 128)], axis=1)
    row_node = lax.broadcasted_iota(jnp.int32, (128, nodes), 0)
    for j in range(nodes // 128):
        unpick_ref[128 * j:128 * (j + 1), :] = (
            row_node == order_row - 128 * j).astype(F32).astype(BF16)
    at_m = lax.broadcasted_iota(jnp.int32, (listed, nblk), 0)
    at_r = lax.broadcasted_iota(jnp.int32, (listed, nblk), 1)
    live_cols = jnp.where(at_m < count_vec[...], cols_vec[...], -1)
    place = at_r * listed + at_m
    for c in range(nblk):
        slots_vec[c:c + 1, :] = jnp.min(
            jnp.where(live_cols == c, place, nblk * listed), axis=0, keepdims=True)
    slot_copy = pltpu.make_async_copy(slots_vec, slots_ref, slot_sem)
    slot_copy.start()
    term_ref[nblk * listed] = zero

    for copy in qk_copies + v_copies:
        copy.wait_recv()
    slot_copy.wait()
    empty = jnp.zeros((half_nodes, BLK), BF16)
    for s in range(seq):
        tile = v_in[s]
        x_ref[nodes_dev * s:nodes_dev * s + half_nodes, 128:] = beside(tile[:, :BLK], empty)
        x_ref[nodes_dev * s + half_nodes:nodes_dev * (s + 1), 128:] = beside(tile[:, BLK:], empty)

    def turned(ref, i, tile):
        swap = pltpu.roll(tile, BLK, 1).astype(BF16)
        tile = tile.astype(BF16)
        ref[0, 2 * i] = jnp.where(low, tile, zero)
        ref[1, 2 * i] = jnp.where(low, zero, swap)
        ref[0, 2 * i + 1] = jnp.where(low, swap, zero)
        ref[1, 2 * i + 1] = jnp.where(low, zero, tile)

    def twice(ref, i, tile):
        ref[2 * i] = tile[:BLK]
        ref[2 * i + 1] = tile[BLK:]

    def into_cluster(i, carry):
        here = pl.ds(pl.multiple_of(i * 128, 128), 128)
        moved = jnp.dot(pick_ref[here, :], x_ref[...], preferred_element_type=F32)
        qk, v = moved[:, :128], moved[:, 128:]
        kq = pltpu.roll(qk, BLK, 1)
        twice(qq_ref, i, (jnp.where(low128, qk, kq) * 0.125).astype(BF16))
        twice(kk_ref, i, jnp.where(low128, kq, qk).astype(BF16))
        twice(vv_ref, i, (v + pltpu.roll(v, BLK, 1)).astype(BF16))
        turned(kt_ref, i, jnp.transpose(qk)[BLK:])
        turned(vt_ref, i, jnp.transpose(v)[:BLK])
        return carry

    lax.fori_loop(0, nodes // 128, into_cluster, 0)

    for i in range(SIDE - 1):
        back = SIDE - 1 - i
        second[2 * i].wait_recv()
        piece = wt_ref.at[lax.rem(y + back, SIDE), :, half_a]
        across.append(push(piece, piece, core_sems, (2, i), mate))
        second[2 * i + 1].wait_recv()
        piece = wt_ref.at[:, lax.rem(x + back, SIDE), half_b]
        across.append(push(piece, piece, core_sems, (3, i), mate))
    loads[4].wait()
    for copy in across:
        copy.wait_recv()
    up_ref[...] = jnp.dot(
        g_ref[...], wt_ref[...].reshape(depth, depth), preferred_element_type=F32).astype(BF16)
    fold(up_ref, b_out)
    b_in[me] = b_out[me]
    b_copies = [
        push(b_out.at[p], b_in.at[me], b_sems, i, (dp, p)) for i, p in enumerate(peers)]

    def diagonal(ref, i):
        blocks = []
        for j in range(4):
            tile = ref[4 * i + j]
            tile = jnp.where(low, tile, zero) if j % 2 == 0 else jnp.where(low, zero, tile)
            blocks.append(beside(tile, zero) if j < 2 else beside(zero, tile))
        return above(*blocks)

    def natural(ref, i, c):
        parts = []
        for m in range(4 * c, 4 * c + 4):
            a, b, d, e = (ref[cols_ref[m, 4 * i + j]] for j in range(4))
            parts.append(beside(jnp.where(low, a, b), jnp.where(low, d, e)))
        return above(*parts)

    def across_keys(ref, i, c):
        parts = []
        for j in range(4):
            r = 4 * i + j
            m = 4 * c
            parts.append(beside(
                ref[0, cols_ref[m, r]] + ref[1, cols_ref[m + 1, r]],
                ref[0, cols_ref[m + 2, r]] + ref[1, cols_ref[m + 3, r]]))
        return above(*parts)

    def diagonal_of(back):
        return beside(
            jnp.where(low, back[:BLK, :128], back[BLK:2 * BLK, :128]),
            jnp.where(low, back[2 * BLK:3 * BLK, 128:], back[3 * BLK:, 128:]))

    lane = lax.broadcasted_iota(jnp.int32, (1, 256), 1)

    def forward(i, carry):
        weights = diagonal(qq_ref, i)
        live = jnp.where(
            lane < 2 * BLK,
            jnp.where(lane < BLK, count_ref[4 * i], count_ref[4 * i + 1]),
            jnp.where(lane < 3 * BLK, count_ref[4 * i + 2], count_ref[4 * i + 3]))
        peak = jnp.full((8, 256), -jnp.inf, F32)
        for c in range(chunks):
            score = lax.dot_general(
                natural(kk_ref, i, c), weights, TRANS_B, preferred_element_type=F32)
            for k in range(4):
                m = 4 * c + k
                part = jnp.where(m < live, score[k * BLK:(k + 1) * BLK], -jnp.inf)
                score_ref[m * BLK:(m + 1) * BLK, :] = part
                peak = jnp.maximum(peak, jnp.max(part.reshape(8, 8, 256), axis=0))
        peak = jnp.max(peak, axis=0, keepdims=True)
        total = jnp.zeros((8, 256), F32)
        for c in range(chunks):
            here = slice(c * 256, (c + 1) * 256)
            terms = jnp.exp(score_ref[here, :] - peak)
            score_ref[here, :] = terms
            total = total + jnp.sum(terms.reshape(32, 8, 256), axis=0)
        inv = 1.0 / jnp.sum(total, axis=0, keepdims=True)
        back = jnp.zeros((256, 256), F32)
        for c in range(chunks):
            here = slice(c * 256, (c + 1) * 256)
            soft = (score_ref[here, :] * inv).astype(BF16)
            soft_ref[i, here, :] = soft
            back = back + jnp.dot(across_keys(vt_ref, i, c), soft, preferred_element_type=F32)
        ot_ref[:, pl.ds(pl.multiple_of(i * 256, 256), 256)] = diagonal_of(back).astype(BF16)
        return carry

    lax.fori_loop(0, quads, forward, 0)

    def outputs_back(j, carry):
        here = pl.ds(pl.multiple_of(j * 128, 128), 128)
        moved = lax.dot_general(
            unpick_ref[here, :], ot_ref[...], TRANS_B, preferred_element_type=F32).astype(BF16)
        o_out[j] = beside(moved[:half_nodes], moved[half_nodes:])
        return carry

    lax.fori_loop(0, seq, outputs_back, 0)
    o_in[me] = o_out[me]
    o_copies = [
        push(o_out.at[p], o_in.at[me], o_sems, i, (dp, p)) for i, p in enumerate(peers)]

    for copy in b_copies:
        copy.wait_recv()
    for s in range(seq):
        tile = b_in[s]
        x_ref[nodes_dev * s:nodes_dev * s + half_nodes, 128:] = beside(
            tile[:, :BLK], tile[:, :BLK])
        x_ref[nodes_dev * s + half_nodes:nodes_dev * (s + 1), 128:] = beside(
            tile[:, BLK:], tile[:, BLK:])

    def upstream_into_cluster(i, carry):
        here = pl.ds(pl.multiple_of(i * 128, 128), 128)
        moved = jnp.dot(pick_ref[here, :], x_ref[:, 128:], preferred_element_type=F32)
        twice(bb_ref, i, moved.astype(BF16))
        bt_ref[:, here] = jnp.transpose(moved)[:BLK]
        return carry

    lax.fori_loop(0, nodes // 128, upstream_into_cluster, 0)

    def backward(i, carry):
        there = pl.ds(pl.multiple_of(i * 256, 256), 256)
        delta = jnp.sum(ot_ref[:, there].astype(F32) * bt_ref[:, there], axis=0, keepdims=True)
        weights = diagonal(bb_ref, i)
        pair_weights = []
        for j in (0, 2):
            q1, q2, b1, b2 = (ref[4 * i + j + k] for ref in (qq_ref, bb_ref) for k in (0, 1))
            pair_weights.append(above(
                beside(jnp.where(low, zero, b1), zero), beside(zero, jnp.where(low, zero, b2)),
                beside(jnp.where(low, q1, zero), zero), beside(zero, jnp.where(low, q2, zero))))
        back = jnp.zeros((256, 256), F32)
        for c in range(chunks):
            here = slice(c * 256, (c + 1) * 256)
            grad = lax.dot_general(
                natural(vv_ref, i, c), weights, TRANS_B, preferred_element_type=F32)
            soft = soft_ref[i, here, :]
            grad = (soft.astype(F32) * (grad - delta)).astype(BF16)
            for j in range(2):
                lanes = slice(128 * j, 128 * (j + 1))
                terms = jnp.dot(
                    beside(soft[:, lanes], grad[:, lanes]), pair_weights[j],
                    preferred_element_type=F32).astype(BF16)
                for k in range(4):
                    m = 4 * c + k
                    slot = (4 * i + 2 * j) * listed + m
                    term_ref[slot] = terms[k * BLK:(k + 1) * BLK, :128]
                    term_ref[slot + listed] = terms[k * BLK:(k + 1) * BLK, 128:]
            back = back + jnp.dot(across_keys(kt_ref, i, c), grad, preferred_element_type=F32)
        grad_q = jnp.transpose(diagonal_of(back) * 0.125).astype(BF16)
        grads_ref[there, 128:] = beside(grad_q, jnp.zeros_like(grad_q))
        return carry

    lax.fori_loop(0, 3, backward, 0)

    for copy in o_copies:
        copy.wait_recv()
    unfold(o_in, attn_ref)
    keep = pl.ds(pl.multiple_of(core * (share // 2), share // 2), share // 2)
    give = pl.ds(pl.multiple_of((1 - core) * (share // 2), share // 2), share // 2)
    mate_copies = []
    for c in range(SIDE):
        part_ref[...] = lax.dot_general(
            g_ref[:, c * SIDE * share:(c + 1) * SIDE * share], attn_ref[...],
            (((0,), (0,)), ((), ())), preferred_element_type=F32).reshape(SIDE, share, depth)
        mate_out[c] = part_ref[:, give, :].astype(BF16)
        sum_ref[c] = part_ref[:, keep, :]
        mate_copies.append(push(mate_out.at[c], mate_in.at[c], mate_sems, c, mate))
    layer_ref[...] = lax.dot_general(
        attn_ref[...], wt_ref[...].reshape(depth, depth), TRANS_B,
        preferred_element_type=F32).astype(BF16)
    for c in range(SIDE):
        mate_copies[c].wait_recv()
        total = sum_ref[c] + mate_in[c].astype(F32)
        sum_ref[c] = total
        half_ref[c] = total.astype(BF16)
    line = []
    for i in range(SIDE - 1):
        line.append(push(
            half_ref.at[:, xs[i], pl.ds(0, rows)], line_in.at[0, i], line_sems, (0, i),
            x_peers[i]))
        line.append(push(
            half_ref.at[ys[i], :, pl.ds(rows, rows)], line_in.at[1, i], line_sems, (1, i),
            y_peers[i]))

    lax.fori_loop(3, quads, backward, 0)

    for copy in line:
        copy.wait_recv()
    sum_a = sum_ref[:, pl.ds(x, 1), :rows, :].reshape(SIDE, rows, depth)
    sum_b = sum_ref[pl.ds(y, 1), :, rows:, :].reshape(SIDE, rows, depth)
    for i in range(SIDE - 1):
        sum_a += line_in[0, i].astype(F32)
        sum_b += line_in[1, i].astype(F32)
    cross_out[0] = sum_a.astype(BF16)
    cross_out[1] = sum_b.astype(BF16)
    cross = []
    for i in range(SIDE - 1):
        cross.append(push(
            cross_out.at[0, ys[i]], cross_in.at[0, i], cross_sems, (0, i), y_peers[i]))
        cross.append(push(
            cross_out.at[1, xs[i]], cross_in.at[1, i], cross_sems, (1, i), x_peers[i]))

    def gather_terms(c, carry):
        total = term_ref[slots_ref[c, 0]].astype(F32)
        for r in range(1, nblk):
            total = total + term_ref[slots_ref[c, r]].astype(F32)
        grads_ref[pl.ds(pl.multiple_of(c * BLK, BLK), BLK), :128] = total.astype(BF16)
        return carry

    lax.fori_loop(0, nblk, gather_terms, 0)

    for copy in cross:
        copy.wait_recv()
    shard_a = cross_out[0, y].astype(F32)
    shard_b = cross_out[1, x].astype(F32)
    for i in range(SIDE - 1):
        shard_a += cross_in[0, i].astype(F32)
        shard_b += cross_in[1, i].astype(F32)
    shard = above(shard_a, shard_b)
    lanes = depth // nz
    for i in range(nz):
        z_out[i] = shard[:, i * lanes:(i + 1) * lanes].astype(BF16)
    z_copies = [
        push(z_out.at[p], z_in.at[i], z_sems, i, (2 * p + core, me))
        for i, p in enumerate(z_peers)]

    def grads_back(j, carry):
        here = pl.ds(pl.multiple_of(j * 128, 128), 128)
        moved = jnp.dot(
            unpick_ref[here, :], grads_ref[...], preferred_element_type=F32).astype(BF16)
        dkv_out[j] = moved[:, :128]
        dq_out[j] = beside(moved[:half_nodes, 128:128 + BLK], moved[half_nodes:, 128:128 + BLK])
        return carry

    lax.fori_loop(0, seq, grads_back, 0)
    dkv_in[me] = dkv_out[me]
    dkv_copies = [
        push(dkv_out.at[p], dkv_in.at[me], dkv_sems, i, (dp, p)) for i, p in enumerate(peers)]
    dq_in[me] = dq_out[me]
    dq_copies = [
        push(dq_out.at[p], dq_in.at[me], dq_sems, i, (dp, p)) for i, p in enumerate(peers)]

    for copy in z_copies:
        copy.wait_recv()
    mine = z_out[z].astype(F32)
    for i in range(nz - 1):
        mine += z_in[i].astype(F32)
    all_in[dp] = mine.astype(BF16)
    all_copies = [
        push(all_in.at[dp], all_in.at[dp], all_sems, i, (p, me))
        for i, p in enumerate(dp_peers)]

    for copy in dkv_copies:
        copy.wait_recv()
    for j in range(seq // 2):
        there = slice(128 * j, 128 * (j + 1))
        a, b = dkv_in[2 * j], dkv_in[2 * j + 1]
        dk_ref[:, there] = beside(a[:, :BLK], b[:, :BLK])
        dv_ref[:, there] = beside(a[:, BLK:], b[:, BLK:])
    for copy in dq_copies:
        copy.wait_recv()
    unfold(dq_in, dq_ref)
    for copy in all_copies:
        copy.wait_recv()
    for i in range(dps):
        wg_ref[i % 2 * (share // 2):(i % 2 + 1) * (share // 2),
               i // 2 * lanes:(i // 2 + 1) * lanes] = all_in[i].astype(F32)
    for copy in (first + second + across + qk_copies + v_copies + b_copies + o_copies
                 + mate_copies + line + cross + z_copies + dkv_copies + dq_copies + all_copies):
        copy.wait_send()


def fused(q, k, v, g, wt, order, cols, count, seq, dps):
    nodes_dev, depth = q.shape
    nodes = seq * nodes_dev
    listed, nblk = cols.shape
    share = depth // seq
    nz = dps // 2
    rows = share // 4
    side = SIDE - 1
    smem = pl.BlockSpec(memory_space=pltpu.SMEM)
    vmem = pl.BlockSpec(memory_space=pltpu.VMEM)
    hbm = pl.BlockSpec(memory_space=pl.ANY)

    def dma(*shape):
        return (pltpu.SemaphoreType.DMA(shape), pltpu.SemaphoreType.DMA(shape))

    flat = jax.ShapeDtypeStruct((nodes_dev, depth), BF16)
    big = pltpu.VMEM((nodes_dev, depth), BF16)
    per_head = pltpu.VMEM((seq, nodes_dev, 128), BF16)
    folded = pltpu.VMEM((seq, nodes_dev // 2, 128), BF16)
    blocks = pltpu.VMEM((nblk, BLK, 128), BF16)
    turned = pltpu.VMEM((2, nblk, BLK, 128), BF16)
    pick = pltpu.VMEM((nodes, nodes), BF16)
    half = pltpu.VMEM((SIDE, SIDE, share // 2, depth), BF16)
    few = max(nz - 1, 1)
    return pl.pallas_call(
        fused_kernel,
        out_shape=(flat, flat, flat, flat, jax.ShapeDtypeStruct((share, depth), F32)),
        in_specs=[smem, smem, vmem, vmem, vmem] + [hbm] * 5,
        out_specs=(vmem,) * 5,
        scratch_shapes=[
            big, big, big, big,
            pltpu.VMEM((SIDE, SIDE, share, depth), BF16),
            big,
            pltpu.VMEM((nblk, nblk), jnp.int32), pltpu.SMEM((nblk, nblk), jnp.int32),
            per_head, folded, folded, pltpu.VMEM((nodes, 256), BF16), folded, folded,
            pick, pick, blocks, blocks, blocks, blocks, turned, turned,
            pltpu.VMEM((BLK, nodes), F32),
            pltpu.VMEM((listed * BLK, 256), F32),
            pltpu.VMEM((nblk // 4, listed * BLK, 256), BF16),
            pltpu.VMEM((BLK, nodes), BF16),
            pltpu.VMEM((nblk * listed + 1, BLK, 128), BF16),
            pltpu.VMEM((nodes, 256), BF16),
            folded, per_head, folded, folded, per_head, folded,
            big,
            pltpu.VMEM((SIDE, share, depth), F32),
            half, half, pltpu.VMEM((SIDE, SIDE, share // 2, depth), F32), half,
            pltpu.VMEM((2, side, SIDE, rows, depth), BF16),
            pltpu.VMEM((2, SIDE, rows, depth), BF16),
            pltpu.VMEM((2, side, rows, depth), BF16),
            pltpu.VMEM((nz, share // 2, depth // nz), BF16),
            pltpu.VMEM((few, share // 2, depth // nz), BF16),
            pltpu.VMEM((dps, share // 2, depth // nz), BF16),
            pltpu.SemaphoreType.DMA((5,)), pltpu.SemaphoreType.DMA,
            dma(2, side), dma(2, side), dma(4, side), dma(seq - 1), dma(seq - 1), dma(seq - 1),
            dma(seq - 1), dma(seq - 1), dma(seq - 1), dma(SIDE), dma(2, side), dma(2, side),
            dma(few), dma(dps - 1),
        ],
        compiler_params=pltpu.CompilerParams(
            collective_id=0, has_side_effects=True, vmem_limit_bytes=62 * 1024 * 1024),
        name="layer",
    )(cols, count, cols, count.reshape(1, nblk), order.reshape(nodes // 128, 128), q, k, v, g, wt)


def finish_kernel(*refs):
    copies = [
        pltpu.make_async_copy(src, dst, refs[-1].at[i])
        for i, (src, dst) in enumerate(zip(refs[:5], refs[5:10]))]
    for copy in copies:
        copy.start()
    for copy in copies:
        copy.wait()


def finish(arrays):
    hbm = pl.BlockSpec(memory_space=pl.ANY)
    return pl.pallas_call(
        finish_kernel,
        out_shape=tuple(jax.ShapeDtypeStruct(a.shape, a.dtype) for a in arrays),
        in_specs=[hbm] * 5,
        out_specs=(hbm,) * 5,
        scratch_shapes=[pltpu.SemaphoreType.DMA((5,))],
        name="finish",
    )(*arrays)


def on_device(queries, key_vectors, value_vectors, out_grad, proj_weight,
              cluster_order, block_cols, block_count):
    seq, dps = lax.axis_size("seq"), lax.axis_size("dp")
    layer, dq, dk, dv, wg = finish(fused(
        queries[0], key_vectors[0], value_vectors[0], out_grad[0], proj_weight.T,
        cluster_order[0], block_cols[0].T, block_count[0], seq, dps))
    return layer[None], dq[None], dk[None], dv[None], wg.T


def solution(mesh):
    rows = P("dp", "seq", None)
    return jax.shard_map(
        on_device,
        mesh=mesh,
        in_specs=(rows, rows, rows, rows, P(None, "seq"),
                  P("dp", None), P("dp", None, None), P("dp", None)),
        out_specs=(rows, rows, rows, rows, P(None, "seq")),
        check_vma=False,
    )
```

```python
import jax
import jax.numpy as jnp
from jax import lax
from jax.experimental import pallas as pl
from jax.experimental.pallas import tpu as pltpu
from jax.sharding import PartitionSpec as P

MESH = pl.DeviceIdType.MESH
SIDE = 4
STEPS = (
    (2, 2), (3, 2), (2, 3), (1, 2), (2, 1), (2, 0), (0, 2), (3, 1), (1, 3), (3, 3), (1, 1),
    (3, 0), (1, 0), (0, 3), (0, 1))
TILE = 512
BLK = 64
F32 = jnp.float32
BF16 = jnp.bfloat16
TRANS_B = (((1,), (1,)), ((), ()))


def push(src, dst, sems, at, device):
    copy = pltpu.make_async_remote_copy(
        src_ref=src, dst_ref=dst, send_sem=sems[0].at[at], recv_sem=sems[1].at[at],
        device_id=device, device_id_type=MESH)
    copy.start()
    return copy


def beside(a, b):
    return jnp.concatenate([a, b], axis=1)


def above(*parts):
    return jnp.concatenate(parts, axis=0)


def fused_kernel(
    cols_ref, count_ref, cols_vec, count_vec, order_ref, q_hbm, k_hbm, v_hbm, g_hbm, w_hbm,
    layer_ref, dq_ref, dk_ref, dv_ref, wg_ref,
    q_ref, k_ref, v_ref, g_ref, gt_ref, wt_ref, up_ref, slots_vec, slots_ref,
    qk_out, v_out, b_out, x_ref, v_in, b_in,
    pick_ref, unpick_ref, qq_ref, kk_ref, vv_ref, bb_ref, kt_ref, vt_ref, bt_ref,
    score_ref, soft_ref, ot_ref, on_ref, term_ref, grads_ref,
    o_out, dkv_out, dq_out, o_in, dkv_in, dq_in,
    attn_ref, part_ref, mate_out, mate_in, sum_ref, half_ref, line_in, cross_out, cross_in,
    z_out, z_in, all_in,
    in_sem, slot_sem, w1_sems, w2_sems, core_sems, qk_sems, v_sems, b_sems,
    o_sems, dkv_sems, dq_sems, mate_sems, line_sems, cross_sems, z_sems, all_sems,
):
    dp, me = lax.axis_index("dp"), lax.axis_index("seq")
    seq, half_nodes, _ = v_out.shape
    nz = all_in.shape[1]
    nodes_dev = 2 * half_nodes
    nodes = seq * nodes_dev
    nblk = nodes // BLK
    listed = cols_ref.shape[0]
    chunks = listed // 4
    quads = nblk // 4
    depth = q_ref.shape[1]
    share = depth // seq
    y, x = me // SIDE, me % SIDE
    core, z = dp % 2, dp // 2
    mate = (dp + 1 - 2 * core, me)
    peers = [lax.rem(y + dy, SIDE) * SIDE + lax.rem(x + dx, SIDE) for dy, dx in STEPS]
    z_peers = [lax.rem(z + i, nz) for i in range(1, nz)]
    xs = [lax.rem(x + i, SIDE) for i in range(1, SIDE)]
    ys = [lax.rem(y + i, SIDE) for i in range(1, SIDE)]
    x_peers = [(dp, y * SIDE + at) for at in xs]
    y_peers = [(dp, at * SIDE + x) for at in ys]
    low128 = lax.broadcasted_iota(jnp.int32, (128, 128), 1) < BLK
    low = lax.broadcasted_iota(jnp.int32, (BLK, 128), 1) < BLK
    zero = jnp.zeros((BLK, 128), BF16)
    zero128 = jnp.zeros((128, 128), BF16)

    loads = [
        pltpu.make_async_copy(src, dst, in_sem.at[i])
        for i, (src, dst) in enumerate((
            (w_hbm, wt_ref.at[y, x]), (k_hbm, k_ref), (q_hbm, q_ref), (v_hbm, v_ref),
            (g_hbm, g_ref)))]
    for load in loads:
        load.start()
    barrier = pltpu.get_barrier_semaphore()
    greeted = [(dp, p) for p in peers] + [(2 * p + core, me) for p in z_peers] + [mate]
    for device in greeted:
        pl.semaphore_signal(barrier, inc=1, device_id=device, device_id_type=MESH)
    pl.semaphore_wait(barrier, len(greeted))

    rows = share // 4
    start_a = pl.multiple_of(core * 2 * rows, 2 * rows)
    half_a = pl.ds(start_a, rows)
    half_b = pl.ds(pl.multiple_of(start_a + rows, rows), rows)
    loads[0].wait()
    first, second, across = [], [], []
    for i in range(SIDE - 1):
        piece = wt_ref.at[y, x, half_a]
        first.append(push(piece, piece, w1_sems, (0, i), x_peers[i]))
        piece = wt_ref.at[y, x, half_b]
        first.append(push(piece, piece, w1_sems, (1, i), y_peers[i]))

    loads[1].wait()
    loads[2].wait()
    for j in range(seq // 2):
        lanes = slice(128 * j, 128 * (j + 1))
        q, k = q_ref[:, lanes], k_ref[:, lanes]
        qk_out[2 * j] = beside(q[:, :BLK], k[:, :BLK])
        qk_out[2 * j + 1] = beside(q[:, BLK:], k[:, BLK:])
    own = pl.ds(pl.multiple_of(me * nodes_dev, nodes_dev), nodes_dev)
    x_ref[own, :128] = qk_out[me]
    qk_copies = [
        push(qk_out.at[p], x_ref.at[own, pl.ds(0, 128)], qk_sems, i, (dp, p))
        for i, p in enumerate(peers)]

    def fold(ref, out):
        for j in range(seq // 2):
            tile = ref[:, 128 * j:128 * (j + 1)]
            out[2 * j] = beside(tile[:half_nodes, :BLK], tile[half_nodes:, :BLK])
            out[2 * j + 1] = beside(tile[:half_nodes, BLK:], tile[half_nodes:, BLK:])

    def unfold(ref, out):
        for j in range(seq // 2):
            lanes = slice(128 * j, 128 * (j + 1))
            a, b = ref[2 * j], ref[2 * j + 1]
            out[:half_nodes, lanes] = beside(a[:, :BLK], b[:, :BLK])
            out[half_nodes:, lanes] = beside(a[:, BLK:], b[:, BLK:])

    loads[3].wait()
    fold(v_ref, v_out)
    v_in[me] = v_out[me]
    v_copies = [
        push(v_out.at[p], v_in.at[me], v_sems, i, (dp, p)) for i, p in enumerate(peers)]

    order = order_ref[...]
    order_col = jnp.transpose(
        above(order.astype(F32), jnp.zeros((128 - order.shape[0], 128), F32))).astype(jnp.int32)
    lane_node = lax.broadcasted_iota(jnp.int32, (128, nodes), 1)
    for i in range(nodes // 128):
        pick_ref[128 * i:128 * (i + 1), :] = (
            lane_node == order_col[:, i:i + 1]).astype(F32).astype(BF16)

    for copy in first:
        copy.wait_recv()
    loads[4].wait()
    for i in range(SIDE - 1):
        piece = wt_ref.at[y, :, half_a]
        second.append(push(piece, piece, w2_sems, (0, i), y_peers[i]))
        piece = wt_ref.at[:, x, half_b]
        second.append(push(piece, piece, w2_sems, (1, i), x_peers[i]))
    for i in range(SIDE - 1):
        piece = wt_ref.at[y, xs[i], half_a]
        across.append(push(piece, piece, core_sems, (0, i), mate))
        piece = wt_ref.at[ys[i], x, half_b]
        across.append(push(piece, piece, core_sems, (1, i), mate))

    for i in range(depth // 128):
        gt_ref[128 * i:128 * (i + 1), :] = jnp.transpose(g_ref[:, 128 * i:128 * (i + 1)])
    order_row = jnp.concatenate([order[i:i + 1, :] for i in range(nodes // 128)], axis=1)
    row_node = lax.broadcasted_iota(jnp.int32, (128, nodes), 0)
    for j in range(nodes // 128):
        unpick_ref[128 * j:128 * (j + 1), :] = (
            row_node == order_row - 128 * j).astype(F32).astype(BF16)
    at_m = lax.broadcasted_iota(jnp.int32, (listed, nblk), 0)
    at_r = lax.broadcasted_iota(jnp.int32, (listed, nblk), 1)
    live_cols = jnp.where(at_m < count_vec[...], cols_vec[...], -1)
    place = at_r * listed + at_m
    for c in range(nblk):
        slots_vec[c:c + 1, :] = jnp.min(
            jnp.where(live_cols == c, place, nblk * listed), axis=0, keepdims=True)
    slot_copy = pltpu.make_async_copy(slots_vec, slots_ref, slot_sem)
    slot_copy.start()
    term_ref[nblk * listed] = zero

    for copy in qk_copies + v_copies:
        copy.wait_recv()
    slot_copy.wait()
    empty = jnp.zeros((half_nodes, BLK), BF16)
    for s in range(seq):
        tile = v_in[s]
        x_ref[nodes_dev * s:nodes_dev * s + half_nodes, 128:] = beside(tile[:, :BLK], empty)
        x_ref[nodes_dev * s + half_nodes:nodes_dev * (s + 1), 128:] = beside(tile[:, BLK:], empty)

    def turned(ref, i, tile):
        swap = pltpu.roll(tile, BLK, 1).astype(BF16)
        tile = tile.astype(BF16)
        ref[0, 2 * i] = jnp.where(low, tile, zero)
        ref[1, 2 * i] = jnp.where(low, zero, swap)
        ref[0, 2 * i + 1] = jnp.where(low, swap, zero)
        ref[1, 2 * i + 1] = jnp.where(low, zero, tile)

    def twice(ref, i, tile):
        ref[2 * i] = tile[:BLK]
        ref[2 * i + 1] = tile[BLK:]

    def into_cluster(t, carry):
        here = pl.ds(pl.multiple_of(t * TILE, TILE), TILE)
        tile = jnp.dot(pick_ref[here, :], x_ref[...], preferred_element_type=F32)
        for k in range(TILE // 128):
            moved = tile[128 * k:128 * (k + 1)]
            i = t * (TILE // 128) + k
            qk, v = moved[:, :128], moved[:, 128:]
            kq = pltpu.roll(qk, BLK, 1)
            twice(qq_ref, i, (jnp.where(low128, qk, kq) * 0.125).astype(BF16))
            twice(kk_ref, i, jnp.where(low128, kq, qk).astype(BF16))
            twice(vv_ref, i, (v + pltpu.roll(v, BLK, 1)).astype(BF16))
            turned(kt_ref, i, jnp.transpose(qk)[BLK:])
            turned(vt_ref, i, jnp.transpose(v)[:BLK])
        return carry

    lax.fori_loop(0, nodes // TILE, into_cluster, 0)

    for i in range(SIDE - 1):
        back = SIDE - 1 - i
        second[2 * i].wait_recv()
        piece = wt_ref.at[lax.rem(y + back, SIDE), :, half_a]
        across.append(push(piece, piece, core_sems, (2, i), mate))
        second[2 * i + 1].wait_recv()
        piece = wt_ref.at[:, lax.rem(x + back, SIDE), half_b]
        across.append(push(piece, piece, core_sems, (3, i), mate))
    for copy in across:
        copy.wait_recv()
    up_ref[...] = jnp.dot(
        g_ref[...], wt_ref[...].reshape(depth, depth), preferred_element_type=F32).astype(BF16)
    fold(up_ref, b_out)
    b_in[me] = b_out[me]
    b_copies = [
        push(b_out.at[p], b_in.at[me], b_sems, i, (dp, p)) for i, p in enumerate(peers)]

    def diagonal(ref, i):
        blocks = []
        for j in range(4):
            tile = ref[4 * i + j]
            tile = jnp.where(low, tile, zero) if j % 2 == 0 else jnp.where(low, zero, tile)
            blocks.append(beside(tile, zero) if j < 2 else beside(zero, tile))
        return above(*blocks)

    def natural(ref, i, c):
        parts = []
        for m in range(4 * c, 4 * c + 4):
            a, b, d, e = (ref[cols_ref[m, 4 * i + j]] for j in range(4))
            parts.append(beside(jnp.where(low, a, b), jnp.where(low, d, e)))
        return above(*parts)

    def across_keys(ref, i, c):
        parts = []
        for j in range(4):
            r = 4 * i + j
            m = 4 * c
            parts.append(beside(
                ref[0, cols_ref[m, r]] + ref[1, cols_ref[m + 1, r]],
                ref[0, cols_ref[m + 2, r]] + ref[1, cols_ref[m + 3, r]]))
        return above(*parts)

    def diagonal_of(back):
        return beside(
            jnp.where(low, back[:BLK, :128], back[BLK:2 * BLK, :128]),
            jnp.where(low, back[2 * BLK:3 * BLK, 128:], back[3 * BLK:, 128:]))

    lane = lax.broadcasted_iota(jnp.int32, (1, 256), 1)

    def forward(i, carry):
        weights = diagonal(qq_ref, i)
        live = jnp.where(
            lane < 2 * BLK,
            jnp.where(lane < BLK, count_ref[4 * i], count_ref[4 * i + 1]),
            jnp.where(lane < 3 * BLK, count_ref[4 * i + 2], count_ref[4 * i + 3]))
        peak = jnp.full((8, 256), -jnp.inf, F32)
        for c in range(chunks):
            score = lax.dot_general(
                natural(kk_ref, i, c), weights, TRANS_B, preferred_element_type=F32)
            for k in range(4):
                m = 4 * c + k
                part = jnp.where(m < live, score[k * BLK:(k + 1) * BLK], -jnp.inf)
                score_ref[m * BLK:(m + 1) * BLK, :] = part
                peak = jnp.maximum(peak, jnp.max(part.reshape(8, 8, 256), axis=0))
        peak = jnp.max(peak, axis=0, keepdims=True)
        total = jnp.zeros((8, 256), F32)
        for c in range(chunks):
            here = slice(c * 256, (c + 1) * 256)
            terms = jnp.exp(score_ref[here, :] - peak)
            score_ref[here, :] = terms
            total = total + jnp.sum(terms.reshape(32, 8, 256), axis=0)
        inv = 1.0 / jnp.sum(total, axis=0, keepdims=True)
        back = jnp.zeros((256, 256), F32)
        for c in range(chunks):
            here = slice(c * 256, (c + 1) * 256)
            soft = (score_ref[here, :] * inv).astype(BF16)
            soft_ref[i, here, :] = soft
            back = back + jnp.dot(across_keys(vt_ref, i, c), soft, preferred_element_type=F32)
        there = pl.ds(pl.multiple_of(i * 256, 256), 256)
        out = diagonal_of(back)
        ot_ref[:, there] = out.astype(BF16)
        out = jnp.transpose(out).astype(BF16)
        on_ref[there, :] = beside(out, jnp.zeros_like(out))
        return carry

    lax.fori_loop(0, quads, forward, 0)

    def fold_rows(tile):
        return beside(tile[:half_nodes, :BLK], tile[half_nodes:, :BLK])

    def back_to_nodes(ref, lanes, out, pack):
        def step(t, carry):
            here = pl.ds(pl.multiple_of(t * TILE, TILE), TILE)
            tile = jnp.dot(
                unpick_ref[here, :], ref[:, lanes], preferred_element_type=F32).astype(BF16)
            for k in range(TILE // 128):
                out[t * (TILE // 128) + k] = pack(tile[128 * k:128 * (k + 1)])
            return carry

        lax.fori_loop(0, nodes // TILE, step, 0)

    back_to_nodes(on_ref, slice(0, 128), o_out, fold_rows)
    o_in[me] = o_out[me]
    o_copies = [
        push(o_out.at[p], o_in.at[me], o_sems, i, (dp, p)) for i, p in enumerate(peers)]

    for copy in b_copies:
        copy.wait_recv()
    for s in range(seq):
        tile = b_in[s]
        x_ref[nodes_dev * s:nodes_dev * s + half_nodes, 128:] = beside(
            tile[:, :BLK], tile[:, :BLK])
        x_ref[nodes_dev * s + half_nodes:nodes_dev * (s + 1), 128:] = beside(
            tile[:, BLK:], tile[:, BLK:])

    def upstream_into_cluster(t, carry):
        here = pl.ds(pl.multiple_of(t * TILE, TILE), TILE)
        tile = jnp.dot(pick_ref[here, :], x_ref[:, 128:], preferred_element_type=F32)
        for k in range(TILE // 128):
            moved = tile[128 * k:128 * (k + 1)]
            i = t * (TILE // 128) + k
            twice(bb_ref, i, moved.astype(BF16))
            bt_ref[:, pl.ds(pl.multiple_of(i * 128, 128), 128)] = jnp.transpose(moved)[:BLK]
        return carry

    lax.fori_loop(0, nodes // TILE, upstream_into_cluster, 0)

    def backward(i, carry):
        there = pl.ds(pl.multiple_of(i * 256, 256), 256)
        delta = jnp.sum(ot_ref[:, there].astype(F32) * bt_ref[:, there], axis=0, keepdims=True)
        weights = diagonal(bb_ref, i)
        pair_weights = []
        for j in (0, 2):
            q1, q2, b1, b2 = (ref[4 * i + j + k] for ref in (qq_ref, bb_ref) for k in (0, 1))
            pair_weights.append(above(
                beside(jnp.where(low, zero, b1), zero), beside(zero, jnp.where(low, zero, b2)),
                beside(jnp.where(low, q1, zero), zero), beside(zero, jnp.where(low, q2, zero))))
        back = jnp.zeros((256, 256), F32)
        for c in range(chunks):
            here = slice(c * 256, (c + 1) * 256)
            grad = lax.dot_general(
                natural(vv_ref, i, c), weights, TRANS_B, preferred_element_type=F32)
            soft = soft_ref[i, here, :]
            grad = (soft.astype(F32) * (grad - delta)).astype(BF16)
            for j in range(2):
                lanes = slice(128 * j, 128 * (j + 1))
                terms = jnp.dot(
                    beside(soft[:, lanes], grad[:, lanes]), pair_weights[j],
                    preferred_element_type=F32).astype(BF16)
                for k in range(4):
                    m = 4 * c + k
                    slot = (4 * i + 2 * j) * listed + m
                    term_ref[slot] = terms[k * BLK:(k + 1) * BLK, :128]
                    term_ref[slot + listed] = terms[k * BLK:(k + 1) * BLK, 128:]
            back = back + jnp.dot(across_keys(kt_ref, i, c), grad, preferred_element_type=F32)
        grad_q = jnp.transpose(diagonal_of(back) * 0.125).astype(BF16)
        grads_ref[there, 128:] = beside(grad_q, jnp.zeros_like(grad_q))
        return carry

    lax.fori_loop(0, 4, backward, 0)

    for copy in o_copies:
        copy.wait_recv()
    unfold(o_in, attn_ref)
    keep = pl.ds(pl.multiple_of(core * (share // 2), share // 2), share // 2)
    give = pl.ds(pl.multiple_of((1 - core) * (share // 2), share // 2), share // 2)
    order_y = ys + [y]
    mate_copies = []
    for c, at in enumerate(order_y):
        there = pl.ds(pl.multiple_of(at * (SIDE * share), SIDE * share), SIDE * share)
        part_ref[...] = jnp.dot(
            gt_ref[there, :], attn_ref[...], preferred_element_type=F32).reshape(
                SIDE, share, depth)
        mate_out[at] = part_ref[:, give, :].astype(BF16)
        sum_ref[at] = part_ref[:, keep, :]
        mate_copies.append(push(mate_out.at[at], mate_in.at[at], mate_sems, c, mate))

    lax.fori_loop(4, 5, backward, 0)

    line_a, line_b = [], []
    for c, at in enumerate(order_y):
        mate_copies[c].wait_recv()
        total = sum_ref[at] + mate_in[at].astype(F32)
        sum_ref[at] = total
        half_ref[at] = total.astype(BF16)
        for i in range(SIDE - 1):
            line_a.append(push(
                half_ref.at[at, xs[i], pl.ds(0, rows)], line_in.at[0, i, at], line_sems, (c, i),
                x_peers[i]))
        if c < SIDE - 1:
            line_b.append(push(
                half_ref.at[at, :, pl.ds(rows, rows)], line_in.at[1, c], line_sems, (SIDE, c),
                y_peers[c]))
    layer_ref[...] = lax.dot_general(
        attn_ref[...], wt_ref[...].reshape(depth, depth), TRANS_B,
        preferred_element_type=F32).astype(BF16)

    lax.fori_loop(5, quads, backward, 0)

    back_to_nodes(grads_ref, slice(128, 256), dq_out, fold_rows)
    dq_in[me] = dq_out[me]
    dq_copies = [
        push(dq_out.at[p], dq_in.at[me], dq_sems, i, (dp, p)) for i, p in enumerate(peers)]

    def gather_terms(c, carry):
        total = term_ref[slots_ref[c, 0]].astype(F32)
        for r in range(1, nblk):
            total = total + term_ref[slots_ref[c, r]].astype(F32)
        grads_ref[pl.ds(pl.multiple_of(c * BLK, BLK), BLK), :128] = total.astype(BF16)
        return carry

    lax.fori_loop(0, nblk, gather_terms, 0)

    for copy in line_a + line_b:
        copy.wait_recv()
    sum_a = sum_ref[:, pl.ds(x, 1), :rows, :].reshape(SIDE, rows, depth)
    sum_b = sum_ref[pl.ds(y, 1), :, rows:, :].reshape(SIDE, rows, depth)
    for i in range(SIDE - 1):
        sum_a += line_in[0, i].astype(F32)
        sum_b += line_in[1, i].astype(F32)
    cross_out[0] = sum_a.astype(BF16)
    cross_out[1] = sum_b.astype(BF16)
    cross = []
    for i in range(SIDE - 1):
        cross.append(push(
            cross_out.at[0, ys[i]], cross_in.at[0, i], cross_sems, (0, i), y_peers[i]))
        cross.append(push(
            cross_out.at[1, xs[i]], cross_in.at[1, i], cross_sems, (1, i), x_peers[i]))

    back_to_nodes(grads_ref, slice(0, 128), dkv_out, lambda tile: tile)
    dkv_in[me] = dkv_out[me]
    dkv_copies = [
        push(dkv_out.at[p], dkv_in.at[me], dkv_sems, i, (dp, p)) for i, p in enumerate(peers)]

    for copy in cross:
        copy.wait_recv()
    shard_a = cross_out[0, y].astype(F32)
    shard_b = cross_out[1, x].astype(F32)
    for i in range(SIDE - 1):
        shard_a += cross_in[0, i].astype(F32)
        shard_b += cross_in[1, i].astype(F32)
    shard = above(shard_a, shard_b)
    lanes = depth // nz
    for i in range(nz):
        z_out[i] = shard[:, i * lanes:(i + 1) * lanes].astype(BF16)
    z_copies = [
        push(z_out.at[p], z_in.at[i], z_sems, i, (2 * p + core, me))
        for i, p in enumerate(z_peers)]
    for copy in dq_copies:
        copy.wait_recv()
    unfold(dq_in, dq_ref)
    for copy in z_copies:
        copy.wait_recv()
    mine = z_out[z].astype(F32)
    for i in range(nz - 1):
        mine += z_in[i].astype(F32)
    all_in[core, z] = mine.astype(BF16)
    all_copies = [
        push(all_in.at[core, z], all_in.at[core, z], all_sems, i, (2 * p + core, me))
        for i, p in enumerate(z_peers)]

    for copy in dkv_copies:
        copy.wait_recv()
    for j in range(seq // 2):
        there = slice(128 * j, 128 * (j + 1))
        a, b = dkv_in[2 * j], dkv_in[2 * j + 1]
        dk_ref[:, there] = beside(a[:, :BLK], b[:, :BLK])
        dv_ref[:, there] = beside(a[:, BLK:], b[:, BLK:])
    for copy in all_copies:
        copy.wait_recv()
    all_copies.append(push(all_in.at[core], all_in.at[core], all_sems, nz - 1, mate))
    all_copies[-1].wait_recv()
    for c in range(2):
        for i in range(nz):
            wg_ref[c * (share // 2):(c + 1) * (share // 2), i * lanes:(i + 1) * lanes] = (
                all_in[c, i].astype(F32))
    for copy in (first + second + across + qk_copies + v_copies + b_copies + o_copies
                 + mate_copies + line_a + line_b + cross + z_copies + dkv_copies + dq_copies
                 + all_copies):
        copy.wait_send()


def fused(q, k, v, g, wt, order, cols, count, seq, dps):
    nodes_dev, depth = q.shape
    nodes = seq * nodes_dev
    listed, nblk = cols.shape
    share = depth // seq
    nz = dps // 2
    rows = share // 4
    side = SIDE - 1
    smem = pl.BlockSpec(memory_space=pltpu.SMEM)
    vmem = pl.BlockSpec(memory_space=pltpu.VMEM)
    hbm = pl.BlockSpec(memory_space=pl.ANY)

    def dma(*shape):
        return (pltpu.SemaphoreType.DMA(shape), pltpu.SemaphoreType.DMA(shape))

    flat = jax.ShapeDtypeStruct((nodes_dev, depth), BF16)
    big = pltpu.VMEM((nodes_dev, depth), BF16)
    per_head = pltpu.VMEM((seq, nodes_dev, 128), BF16)
    folded = pltpu.VMEM((seq, nodes_dev // 2, 128), BF16)
    blocks = pltpu.VMEM((nblk, BLK, 128), BF16)
    turned = pltpu.VMEM((2, nblk, BLK, 128), BF16)
    pick = pltpu.VMEM((nodes, nodes), BF16)
    half = pltpu.VMEM((SIDE, SIDE, share // 2, depth), BF16)
    few = max(nz - 1, 1)
    return pl.pallas_call(
        fused_kernel,
        out_shape=(flat, flat, flat, flat, jax.ShapeDtypeStruct((share, depth), F32)),
        in_specs=[smem, smem, vmem, vmem, vmem] + [hbm] * 5,
        out_specs=(vmem,) * 5,
        scratch_shapes=[
            big, big, big, big, pltpu.VMEM((depth, nodes_dev), BF16),
            pltpu.VMEM((SIDE, SIDE, share, depth), BF16),
            big,
            pltpu.VMEM((nblk, nblk), jnp.int32), pltpu.SMEM((nblk, nblk), jnp.int32),
            per_head, folded, folded, pltpu.VMEM((nodes, 256), BF16), folded, folded,
            pick, pick, blocks, blocks, blocks, blocks, turned, turned,
            pltpu.VMEM((BLK, nodes), F32),
            pltpu.VMEM((listed * BLK, 256), F32),
            pltpu.VMEM((nblk // 4, listed * BLK, 256), BF16),
            pltpu.VMEM((BLK, nodes), BF16),
            pltpu.VMEM((nodes, 128), BF16),
            pltpu.VMEM((nblk * listed + 1, BLK, 128), BF16),
            pltpu.VMEM((nodes, 256), BF16),
            folded, per_head, folded, folded, per_head, folded,
            big,
            pltpu.VMEM((SIDE, share, depth), F32),
            half, half, pltpu.VMEM((SIDE, SIDE, share // 2, depth), F32), half,
            pltpu.VMEM((2, side, SIDE, rows, depth), BF16),
            pltpu.VMEM((2, SIDE, rows, depth), BF16),
            pltpu.VMEM((2, side, rows, depth), BF16),
            pltpu.VMEM((nz, share // 2, depth // nz), BF16),
            pltpu.VMEM((few, share // 2, depth // nz), BF16),
            pltpu.VMEM((2, nz, share // 2, depth // nz), BF16),
            pltpu.SemaphoreType.DMA((5,)), pltpu.SemaphoreType.DMA,
            dma(2, side), dma(2, side), dma(4, side), dma(seq - 1), dma(seq - 1), dma(seq - 1),
            dma(seq - 1), dma(seq - 1), dma(seq - 1), dma(SIDE), dma(SIDE + 1, side), dma(2, side),
            dma(few), dma(nz),
        ],
        compiler_params=pltpu.CompilerParams(
            collective_id=0, has_side_effects=True, vmem_limit_bytes=62 * 1024 * 1024),
        name="layer",
    )(cols, count, cols, count.reshape(1, nblk), order.reshape(nodes // 128, 128), q, k, v, g, wt)


def finish_kernel(*refs):
    arrays, outs, held, (load_sem, store_sem) = refs[:5], refs[5:10], refs[10:15], refs[15:]
    loads = [
        pltpu.make_async_copy(src, dst, load_sem.at[i])
        for i, (src, dst) in enumerate(zip(arrays, held))]
    stores = [
        pltpu.make_async_copy(src, dst, store_sem.at[i])
        for i, (src, dst) in enumerate(zip(held, outs))]
    for load in loads:
        load.start()
    for load, store in zip(loads, stores):
        load.wait()
        store.start()
    for store in stores:
        store.wait()


def finish(arrays):
    hbm = pl.BlockSpec(memory_space=pl.ANY)
    return pl.pallas_call(
        finish_kernel,
        out_shape=tuple(jax.ShapeDtypeStruct(a.shape, a.dtype) for a in arrays),
        in_specs=[hbm] * 5,
        out_specs=(hbm,) * 5,
        scratch_shapes=[pltpu.VMEM(a.shape, a.dtype) for a in arrays]
        + [pltpu.SemaphoreType.DMA((5,)), pltpu.SemaphoreType.DMA((5,))],
        compiler_params=pltpu.CompilerParams(vmem_limit_bytes=62 * 1024 * 1024),
        name="finish",
    )(*arrays)


def on_device(queries, key_vectors, value_vectors, out_grad, proj_weight,
              cluster_order, block_cols, block_count):
    seq, dps = lax.axis_size("seq"), lax.axis_size("dp")
    layer, dq, dk, dv, wg = finish(fused(
        queries[0], key_vectors[0], value_vectors[0], out_grad[0], proj_weight.T,
        cluster_order[0], block_cols[0].T, block_count[0], seq, dps))
    return layer[None], dq[None], dk[None], dv[None], wg.T


def solution(mesh):
    rows = P("dp", "seq", None)
    return jax.shard_map(
        on_device,
        mesh=mesh,
        in_specs=(rows, rows, rows, rows, P(None, "seq"),
                  P("dp", None), P("dp", None, None), P("dp", None)),
        out_specs=(rows, rows, rows, rows, P(None, "seq")),
        check_vma=False,
    )
```

```python
import jax
import jax.numpy as jnp
from jax import lax
from jax.experimental import pallas as pl
from jax.experimental.pallas import tpu as pltpu
from jax.sharding import PartitionSpec as P

MESH = pl.DeviceIdType.MESH
SIDE = 4
STEPS = (
    (2, 2), (3, 2), (2, 3), (1, 2), (2, 1), (2, 0), (0, 2), (3, 1), (1, 3), (3, 3), (1, 1),
    (3, 0), (1, 0), (0, 3), (0, 1))
TILE = 1024
BLK = 64
F32 = jnp.float32
BF16 = jnp.bfloat16
TRANS_B = (((1,), (1,)), ((), ()))


def push(src, dst, sems, at, device):
    copy = pltpu.make_async_remote_copy(
        src_ref=src, dst_ref=dst, send_sem=sems[0].at[at], recv_sem=sems[1].at[at],
        device_id=device, device_id_type=MESH)
    copy.start()
    return copy


def beside(a, b):
    return jnp.concatenate([a, b], axis=1)


def above(*parts):
    return jnp.concatenate(parts, axis=0)


def fused_kernel(
    cols_ref, count_ref, cols_vec, count_vec, order_ref, q_hbm, k_hbm, v_hbm, g_hbm, w_hbm,
    layer_ref, dq_ref, dk_ref, dv_ref, wg_ref,
    q_ref, k_ref, v_ref, g_ref, gt_ref, wt_ref, up_ref, slots_vec, slots_ref,
    qk_out, v_out, b_out, x_ref, v_in, b_in,
    pick_ref, unpick_ref, qq_ref, kk_ref, vv_ref, bb_ref, kt_ref, vt_ref, bt_ref,
    score_ref, inv_ref, soft_ref, ot_ref, on_ref, term_ref, grads_ref,
    o_out, dkv_out, dq_out, o_in, dkv_in, dq_in,
    attn_ref, part_ref, mate_out, mate_in, sum_ref, half_ref, line_in, cross_out, cross_in,
    z_out, z_in, all_in,
    in_sem, slot_sem, w1_sems, w2_sems, core_sems, qk_sems, v_sems, b_sems,
    o_sems, dkv_sems, dq_sems, mate_sems, line_sems, cross_sems, z_sems, all_sems,
):
    dp, me = lax.axis_index("dp"), lax.axis_index("seq")
    seq, half_nodes, _ = v_out.shape
    nz = all_in.shape[1]
    nodes_dev = 2 * half_nodes
    nodes = seq * nodes_dev
    nblk = nodes // BLK
    listed = cols_ref.shape[0]
    chunks = listed // 4
    quads = nblk // 4
    depth = q_ref.shape[1]
    share = depth // seq
    y, x = me // SIDE, me % SIDE
    core, z = dp % 2, dp // 2
    mate = (dp + 1 - 2 * core, me)
    peers = [lax.rem(y + dy, SIDE) * SIDE + lax.rem(x + dx, SIDE) for dy, dx in STEPS]
    z_peers = [lax.rem(z + i, nz) for i in range(1, nz)]
    xs = [lax.rem(x + i, SIDE) for i in range(1, SIDE)]
    ys = [lax.rem(y + i, SIDE) for i in range(1, SIDE)]
    x_peers = [(dp, y * SIDE + at) for at in xs]
    y_peers = [(dp, at * SIDE + x) for at in ys]
    low128 = lax.broadcasted_iota(jnp.int32, (128, 128), 1) < BLK
    low = lax.broadcasted_iota(jnp.int32, (BLK, 128), 1) < BLK
    zero = jnp.zeros((BLK, 128), BF16)
    zero128 = jnp.zeros((128, 128), BF16)

    loads = [
        pltpu.make_async_copy(src, dst, in_sem.at[i])
        for i, (src, dst) in enumerate((
            (w_hbm, wt_ref.at[y, x]), (k_hbm, k_ref), (q_hbm, q_ref), (v_hbm, v_ref),
            (g_hbm, g_ref)))]
    for load in loads:
        load.start()
    barrier = pltpu.get_barrier_semaphore()
    greeted = [(dp, p) for p in peers] + [(2 * p + core, me) for p in z_peers] + [mate]
    for device in greeted:
        pl.semaphore_signal(barrier, inc=1, device_id=device, device_id_type=MESH)
    pl.semaphore_wait(barrier, len(greeted))

    rows = share // 4
    start_a = pl.multiple_of(core * 2 * rows, 2 * rows)
    half_a = pl.ds(start_a, rows)
    half_b = pl.ds(pl.multiple_of(start_a + rows, rows), rows)
    loads[0].wait()
    first, second, across = [], [], []
    for i in range(SIDE - 1):
        piece = wt_ref.at[y, x, half_a]
        first.append(push(piece, piece, w1_sems, (0, i), x_peers[i]))
        piece = wt_ref.at[y, x, half_b]
        first.append(push(piece, piece, w1_sems, (1, i), y_peers[i]))

    loads[1].wait()
    loads[2].wait()
    for j in range(seq // 2):
        lanes = slice(128 * j, 128 * (j + 1))
        q, k = q_ref[:, lanes], k_ref[:, lanes]
        qk_out[2 * j] = beside(q[:, :BLK], k[:, :BLK])
        qk_out[2 * j + 1] = beside(q[:, BLK:], k[:, BLK:])
    own = pl.ds(pl.multiple_of(me * nodes_dev, nodes_dev), nodes_dev)
    x_ref[own, :128] = qk_out[me]
    qk_copies = [
        push(qk_out.at[p], x_ref.at[own, pl.ds(0, 128)], qk_sems, i, (dp, p))
        for i, p in enumerate(peers)]

    def fold(ref, out):
        for j in range(seq // 2):
            tile = ref[:, 128 * j:128 * (j + 1)]
            out[2 * j] = beside(tile[:half_nodes, :BLK], tile[half_nodes:, :BLK])
            out[2 * j + 1] = beside(tile[:half_nodes, BLK:], tile[half_nodes:, BLK:])

    def unfold(ref, out):
        for j in range(seq // 2):
            lanes = slice(128 * j, 128 * (j + 1))
            a, b = ref[2 * j], ref[2 * j + 1]
            out[:half_nodes, lanes] = beside(a[:, :BLK], b[:, :BLK])
            out[half_nodes:, lanes] = beside(a[:, BLK:], b[:, BLK:])

    loads[3].wait()
    fold(v_ref, v_out)
    v_in[me] = v_out[me]
    v_copies = [
        push(v_out.at[p], v_in.at[me], v_sems, i, (dp, p)) for i, p in enumerate(peers)]

    order = order_ref[...]
    order_col = jnp.transpose(
        above(order.astype(F32), jnp.zeros((128 - order.shape[0], 128), F32))).astype(jnp.int32)
    lane_node = lax.broadcasted_iota(jnp.int32, (128, nodes), 1)
    for i in range(nodes // 128):
        pick_ref[128 * i:128 * (i + 1), :] = (
            lane_node == order_col[:, i:i + 1]).astype(F32).astype(BF16)

    for copy in first:
        copy.wait_recv()
    loads[4].wait()
    for i in range(SIDE - 1):
        piece = wt_ref.at[y, :, half_a]
        second.append(push(piece, piece, w2_sems, (0, i), y_peers[i]))
        piece = wt_ref.at[:, x, half_b]
        second.append(push(piece, piece, w2_sems, (1, i), x_peers[i]))
    for i in range(SIDE - 1):
        piece = wt_ref.at[y, xs[i], half_a]
        across.append(push(piece, piece, core_sems, (0, i), mate))
        piece = wt_ref.at[ys[i], x, half_b]
        across.append(push(piece, piece, core_sems, (1, i), mate))

    for i in range(depth // 128):
        gt_ref[128 * i:128 * (i + 1), :] = jnp.transpose(g_ref[:, 128 * i:128 * (i + 1)])
    order_row = jnp.concatenate([order[i:i + 1, :] for i in range(nodes // 128)], axis=1)
    row_node = lax.broadcasted_iota(jnp.int32, (128, nodes), 0)
    for j in range(nodes // 128):
        unpick_ref[128 * j:128 * (j + 1), :] = (
            row_node == order_row - 128 * j).astype(F32).astype(BF16)
    at_m = lax.broadcasted_iota(jnp.int32, (listed, nblk), 0)
    at_r = lax.broadcasted_iota(jnp.int32, (listed, nblk), 1)
    live_cols = jnp.where(at_m < count_vec[...], cols_vec[...], -1)
    place = at_r * listed + at_m
    for c in range(nblk):
        slots_vec[c:c + 1, :] = jnp.min(
            jnp.where(live_cols == c, place, nblk * listed), axis=0, keepdims=True)
    slot_copy = pltpu.make_async_copy(slots_vec, slots_ref, slot_sem)
    slot_copy.start()
    term_ref[nblk * listed] = zero

    for copy in qk_copies + v_copies:
        copy.wait_recv()
    slot_copy.wait()
    empty = jnp.zeros((half_nodes, BLK), BF16)
    for s in range(seq):
        tile = v_in[s]
        x_ref[nodes_dev * s:nodes_dev * s + half_nodes, 128:] = beside(tile[:, :BLK], empty)
        x_ref[nodes_dev * s + half_nodes:nodes_dev * (s + 1), 128:] = beside(tile[:, BLK:], empty)

    def turned(ref, i, tile):
        swap = pltpu.roll(tile, BLK, 1).astype(BF16)
        tile = tile.astype(BF16)
        ref[0, 2 * i] = jnp.where(low, tile, zero)
        ref[1, 2 * i] = jnp.where(low, zero, swap)
        ref[0, 2 * i + 1] = jnp.where(low, swap, zero)
        ref[1, 2 * i + 1] = jnp.where(low, zero, tile)

    def twice(ref, i, tile):
        ref[2 * i] = tile[:BLK]
        ref[2 * i + 1] = tile[BLK:]

    def into_cluster(t, carry):
        here = pl.ds(pl.multiple_of(t * TILE, TILE), TILE)
        tile = jnp.dot(pick_ref[here, :], x_ref[...], preferred_element_type=F32)
        for k in range(TILE // 128):
            moved = tile[128 * k:128 * (k + 1)]
            i = t * (TILE // 128) + k
            qk, v = moved[:, :128], moved[:, 128:]
            kq = pltpu.roll(qk, BLK, 1)
            twice(qq_ref, i, (jnp.where(low128, qk, kq) * 0.125).astype(BF16))
            twice(kk_ref, i, jnp.where(low128, kq, qk).astype(BF16))
            twice(vv_ref, i, (v + pltpu.roll(v, BLK, 1)).astype(BF16))
            turned(kt_ref, i, jnp.transpose(qk)[BLK:])
            turned(vt_ref, i, jnp.transpose(v)[:BLK])
        return carry

    lax.fori_loop(0, nodes // TILE, into_cluster, 0)

    for i in range(SIDE - 1):
        back = SIDE - 1 - i
        second[2 * i].wait_recv()
        piece = wt_ref.at[lax.rem(y + back, SIDE), :, half_a]
        across.append(push(piece, piece, core_sems, (2, i), mate))
        second[2 * i + 1].wait_recv()
        piece = wt_ref.at[:, lax.rem(x + back, SIDE), half_b]
        across.append(push(piece, piece, core_sems, (3, i), mate))
    for copy in across:
        copy.wait_recv()
    up_ref[...] = jnp.dot(
        g_ref[...], wt_ref[...].reshape(depth, depth), preferred_element_type=F32).astype(BF16)
    fold(up_ref, b_out)
    b_in[me] = b_out[me]
    b_copies = [
        push(b_out.at[p], b_in.at[me], b_sems, i, (dp, p)) for i, p in enumerate(peers)]

    def diagonal(ref, i):
        blocks = []
        for j in range(4):
            tile = ref[4 * i + j]
            tile = jnp.where(low, tile, zero) if j % 2 == 0 else jnp.where(low, zero, tile)
            blocks.append(beside(tile, zero) if j < 2 else beside(zero, tile))
        return above(*blocks)

    def natural(ref, i, c):
        parts = []
        for m in range(4 * c, 4 * c + 4):
            a, b, d, e = (ref[cols_ref[m, 4 * i + j]] for j in range(4))
            parts.append(beside(jnp.where(low, a, b), jnp.where(low, d, e)))
        return above(*parts)

    def across_keys(ref, i, c):
        parts = []
        for j in range(4):
            r = 4 * i + j
            m = 4 * c
            parts.append(beside(
                ref[0, cols_ref[m, r]] + ref[1, cols_ref[m + 1, r]],
                ref[0, cols_ref[m + 2, r]] + ref[1, cols_ref[m + 3, r]]))
        return above(*parts)

    def diagonal_of(back):
        return beside(
            jnp.where(low, back[:BLK, :128], back[BLK:2 * BLK, :128]),
            jnp.where(low, back[2 * BLK:3 * BLK, 128:], back[3 * BLK:, 128:]))

    lane = lax.broadcasted_iota(jnp.int32, (1, 256), 1)

    def live_of(i):
        return jnp.where(
            lane < 2 * BLK,
            jnp.where(lane < BLK, count_ref[4 * i], count_ref[4 * i + 1]),
            jnp.where(lane < 3 * BLK, count_ref[4 * i + 2], count_ref[4 * i + 3]))

    def scores(i, c, weights, live, held, peak):
        score = lax.dot_general(
            natural(kk_ref, i, c), weights, TRANS_B, preferred_element_type=F32)
        for k in range(4):
            m = 4 * c + k
            part = jnp.where(m < live, score[k * BLK:(k + 1) * BLK], -jnp.inf)
            score_ref[held, m * BLK:(m + 1) * BLK, :] = part
            peak = jnp.maximum(peak, jnp.max(part.reshape(8, 8, 256), axis=0))
        return peak

    no_peak = jnp.full((8, 256), -jnp.inf, F32)

    def forward_step(i, held, peak):
        after = jnp.minimum(i + 1, quads - 1)
        weights, live = diagonal(qq_ref, after), live_of(after)
        peak = jnp.max(peak, axis=0, keepdims=True)
        total = jnp.zeros((8, 256), F32)
        back = jnp.zeros((256, 256), F32)
        next_peak = no_peak
        for c in range(chunks):
            next_peak = scores(after, c, weights, live, 1 - held, next_peak)
            here = slice(c * 256, (c + 1) * 256)
            terms = jnp.exp(score_ref[held, here, :] - peak)
            total = total + jnp.sum(terms.reshape(32, 8, 256), axis=0)
            terms = terms.astype(BF16)
            soft_ref[i, here, :] = terms
            back = back + jnp.dot(across_keys(vt_ref, i, c), terms, preferred_element_type=F32)
        inv = 1.0 / jnp.sum(total, axis=0, keepdims=True)
        there = pl.ds(pl.multiple_of(i * 256, 256), 256)
        inv_ref[:, there] = inv
        out = diagonal_of(back) * inv
        ot_ref[:, there] = out.astype(BF16)
        out = jnp.transpose(out).astype(BF16)
        on_ref[there, :] = beside(out, jnp.zeros_like(out))
        return next_peak

    def forward(i, peak):
        peak = forward_step(2 * i, 0, peak)
        return forward_step(2 * i + 1, 1, peak)

    def first_scores():
        peak = no_peak
        weights, live = diagonal(qq_ref, 0), live_of(0)
        for c in range(chunks):
            peak = scores(0, c, weights, live, 0, peak)
        return peak

    lax.fori_loop(0, quads // 2, forward, first_scores())

    def fold_rows(tile):
        return beside(tile[:half_nodes, :BLK], tile[half_nodes:, :BLK])

    def back_to_nodes(ref, lanes, out, pack):
        def step(t, carry):
            here = pl.ds(pl.multiple_of(t * TILE, TILE), TILE)
            tile = jnp.dot(
                unpick_ref[here, :], ref[:, lanes], preferred_element_type=F32).astype(BF16)
            for k in range(TILE // 128):
                out[t * (TILE // 128) + k] = pack(tile[128 * k:128 * (k + 1)])
            return carry

        lax.fori_loop(0, nodes // TILE, step, 0)

    back_to_nodes(on_ref, slice(0, 128), o_out, fold_rows)
    o_in[me] = o_out[me]
    o_copies = [
        push(o_out.at[p], o_in.at[me], o_sems, i, (dp, p)) for i, p in enumerate(peers)]

    for copy in b_copies:
        copy.wait_recv()
    for s in range(seq):
        tile = b_in[s]
        x_ref[nodes_dev * s:nodes_dev * s + half_nodes, 128:] = beside(
            tile[:, :BLK], tile[:, :BLK])
        x_ref[nodes_dev * s + half_nodes:nodes_dev * (s + 1), 128:] = beside(
            tile[:, BLK:], tile[:, BLK:])

    def upstream_into_cluster(t, carry):
        here = pl.ds(pl.multiple_of(t * TILE, TILE), TILE)
        tile = jnp.dot(pick_ref[here, :], x_ref[:, 128:], preferred_element_type=F32)
        for k in range(TILE // 128):
            moved = tile[128 * k:128 * (k + 1)]
            i = t * (TILE // 128) + k
            twice(bb_ref, i, moved.astype(BF16))
            bt_ref[:, pl.ds(pl.multiple_of(i * 128, 128), 128)] = jnp.transpose(moved)[:BLK]
        return carry

    lax.fori_loop(0, nodes // TILE, upstream_into_cluster, 0)

    def backward(i, carry):
        there = pl.ds(pl.multiple_of(i * 256, 256), 256)
        delta = jnp.sum(ot_ref[:, there].astype(F32) * bt_ref[:, there], axis=0, keepdims=True)
        weights = diagonal(bb_ref, i)
        pair_weights = []
        for j in (0, 2):
            q1, q2, b1, b2 = (ref[4 * i + j + k] for ref in (qq_ref, bb_ref) for k in (0, 1))
            pair_weights.append(above(
                beside(jnp.where(low, zero, b1), zero), beside(zero, jnp.where(low, zero, b2)),
                beside(jnp.where(low, q1, zero), zero), beside(zero, jnp.where(low, q2, zero))))
        inv = inv_ref[:, there]

        def grad_soft(c):
            return lax.dot_general(
                natural(vv_ref, i, c), weights, TRANS_B, preferred_element_type=F32)

        back = jnp.zeros((256, 256), F32)
        grad = grad_soft(0)
        for c in range(chunks):
            here = slice(c * 256, (c + 1) * 256)
            ahead = grad_soft(c + 1) if c + 1 < chunks else None
            soft = soft_ref[i, here, :].astype(F32) * inv
            grad = (soft * (grad - delta)).astype(BF16)
            soft = soft.astype(BF16)
            for j in range(2):
                lanes = slice(128 * j, 128 * (j + 1))
                terms = jnp.dot(
                    beside(soft[:, lanes], grad[:, lanes]), pair_weights[j],
                    preferred_element_type=F32).astype(BF16)
                for k in range(4):
                    m = 4 * c + k
                    slot = (4 * i + 2 * j) * listed + m
                    term_ref[slot] = terms[k * BLK:(k + 1) * BLK, :128]
                    term_ref[slot + listed] = terms[k * BLK:(k + 1) * BLK, 128:]
            back = back + jnp.dot(across_keys(kt_ref, i, c), grad, preferred_element_type=F32)
            grad = ahead
        grad_q = jnp.transpose(diagonal_of(back) * 0.125).astype(BF16)
        grads_ref[there, 128:] = beside(grad_q, jnp.zeros_like(grad_q))
        return carry

    def backward_pair(i, carry):
        return backward(2 * i + 1, backward(2 * i, carry))

    lax.fori_loop(0, 2, backward_pair, 0)

    for copy in o_copies:
        copy.wait_recv()
    unfold(o_in, attn_ref)
    keep = pl.ds(pl.multiple_of(core * (share // 2), share // 2), share // 2)
    give = pl.ds(pl.multiple_of((1 - core) * (share // 2), share // 2), share // 2)
    order_y = ys + [y]
    mate_copies = []
    for c, at in enumerate(order_y):
        there = pl.ds(pl.multiple_of(at * (SIDE * share), SIDE * share), SIDE * share)
        part_ref[...] = jnp.dot(
            gt_ref[there, :], attn_ref[...], preferred_element_type=F32).reshape(
                SIDE, share, depth)
        mate_out[at] = part_ref[:, give, :].astype(BF16)
        sum_ref[at] = part_ref[:, keep, :]
        mate_copies.append(push(mate_out.at[at], mate_in.at[at], mate_sems, c, mate))

    lax.fori_loop(2, 3, backward_pair, 0)

    line_a, line_b = [], []
    for c, at in enumerate(order_y):
        mate_copies[c].wait_recv()
        total = sum_ref[at] + mate_in[at].astype(F32)
        sum_ref[at] = total
        half_ref[at] = total.astype(BF16)
        for i in range(SIDE - 1):
            line_a.append(push(
                half_ref.at[at, xs[i], pl.ds(0, rows)], line_in.at[0, i, at], line_sems, (c, i),
                x_peers[i]))
        if c < SIDE - 1:
            line_b.append(push(
                half_ref.at[at, :, pl.ds(rows, rows)], line_in.at[1, c], line_sems, (SIDE, c),
                y_peers[c]))
    layer_ref[...] = lax.dot_general(
        attn_ref[...], wt_ref[...].reshape(depth, depth), TRANS_B,
        preferred_element_type=F32).astype(BF16)

    lax.fori_loop(3, quads // 2, backward_pair, 0)

    back_to_nodes(grads_ref, slice(128, 256), dq_out, fold_rows)
    dq_in[me] = dq_out[me]
    dq_copies = [
        push(dq_out.at[p], dq_in.at[me], dq_sems, i, (dp, p)) for i, p in enumerate(peers)]

    def gather_terms(c, carry):
        total = jnp.zeros((BLK, 128), F32)
        for r in range(0, nblk, 2):
            pair = term_ref[slots_ref[c, r]] + term_ref[slots_ref[c, r + 1]]
            total = total + pair.astype(F32)
        grads_ref[pl.ds(pl.multiple_of(c * BLK, BLK), BLK), :128] = total.astype(BF16)
        return carry

    lax.fori_loop(0, nblk, gather_terms, 0)

    for copy in line_a + line_b:
        copy.wait_recv()
    sum_a = sum_ref[:, pl.ds(x, 1), :rows, :].reshape(SIDE, rows, depth)
    sum_b = sum_ref[pl.ds(y, 1), :, rows:, :].reshape(SIDE, rows, depth)
    for i in range(SIDE - 1):
        sum_a += line_in[0, i].astype(F32)
        sum_b += line_in[1, i].astype(F32)
    cross_out[0] = sum_a.astype(BF16)
    cross_out[1] = sum_b.astype(BF16)
    cross = []
    for i in range(SIDE - 1):
        cross.append(push(
            cross_out.at[0, ys[i]], cross_in.at[0, i], cross_sems, (0, i), y_peers[i]))
        cross.append(push(
            cross_out.at[1, xs[i]], cross_in.at[1, i], cross_sems, (1, i), x_peers[i]))

    back_to_nodes(grads_ref, slice(0, 128), dkv_out, lambda tile: tile)
    dkv_in[me] = dkv_out[me]
    dkv_copies = [
        push(dkv_out.at[p], dkv_in.at[me], dkv_sems, i, (dp, p)) for i, p in enumerate(peers)]

    for copy in cross:
        copy.wait_recv()
    shard_a = cross_out[0, y].astype(F32)
    shard_b = cross_out[1, x].astype(F32)
    for i in range(SIDE - 1):
        shard_a += cross_in[0, i].astype(F32)
        shard_b += cross_in[1, i].astype(F32)
    shard = above(shard_a, shard_b)
    lanes = depth // nz
    for i in range(nz):
        z_out[i] = shard[:, i * lanes:(i + 1) * lanes].astype(BF16)
    z_copies = [
        push(z_out.at[p], z_in.at[i], z_sems, i, (2 * p + core, me))
        for i, p in enumerate(z_peers)]
    for copy in dq_copies:
        copy.wait_recv()
    unfold(dq_in, dq_ref)
    for copy in z_copies:
        copy.wait_recv()
    mine = z_out[z].astype(F32)
    for i in range(nz - 1):
        mine += z_in[i].astype(F32)
    all_in[core, z] = mine.astype(BF16)
    all_copies = [
        push(all_in.at[core, z], all_in.at[core, z], all_sems, i, (2 * p + core, me))
        for i, p in enumerate(z_peers)]

    for copy in dkv_copies:
        copy.wait_recv()
    for j in range(seq // 2):
        there = slice(128 * j, 128 * (j + 1))
        a, b = dkv_in[2 * j], dkv_in[2 * j + 1]
        dk_ref[:, there] = beside(a[:, :BLK], b[:, :BLK])
        dv_ref[:, there] = beside(a[:, BLK:], b[:, BLK:])
    for copy in all_copies:
        copy.wait_recv()
    all_copies.append(push(all_in.at[core], all_in.at[core], all_sems, nz - 1, mate))
    all_copies[-1].wait_recv()
    for c in range(2):
        for i in range(nz):
            wg_ref[c * (share // 2):(c + 1) * (share // 2), i * lanes:(i + 1) * lanes] = (
                all_in[c, i].astype(F32))
    for copy in (first + second + across + qk_copies + v_copies + b_copies + o_copies
                 + mate_copies + line_a + line_b + cross + z_copies + dkv_copies + dq_copies
                 + all_copies):
        copy.wait_send()


def fused(q, k, v, g, wt, order, cols, count, seq, dps):
    nodes_dev, depth = q.shape
    nodes = seq * nodes_dev
    listed, nblk = cols.shape
    share = depth // seq
    nz = dps // 2
    rows = share // 4
    side = SIDE - 1
    smem = pl.BlockSpec(memory_space=pltpu.SMEM)
    vmem = pl.BlockSpec(memory_space=pltpu.VMEM)
    hbm = pl.BlockSpec(memory_space=pl.ANY)

    def dma(*shape):
        return (pltpu.SemaphoreType.DMA(shape), pltpu.SemaphoreType.DMA(shape))

    flat = jax.ShapeDtypeStruct((nodes_dev, depth), BF16)
    big = pltpu.VMEM((nodes_dev, depth), BF16)
    per_head = pltpu.VMEM((seq, nodes_dev, 128), BF16)
    folded = pltpu.VMEM((seq, nodes_dev // 2, 128), BF16)
    blocks = pltpu.VMEM((nblk, BLK, 128), BF16)
    turned = pltpu.VMEM((2, nblk, BLK, 128), BF16)
    pick = pltpu.VMEM((nodes, nodes), BF16)
    half = pltpu.VMEM((SIDE, SIDE, share // 2, depth), BF16)
    few = max(nz - 1, 1)
    return pl.pallas_call(
        fused_kernel,
        out_shape=(flat, flat, flat, flat, jax.ShapeDtypeStruct((share, depth), F32)),
        in_specs=[smem, smem, vmem, vmem, vmem] + [hbm] * 5,
        out_specs=(vmem,) * 5,
        scratch_shapes=[
            big, big, big, big, pltpu.VMEM((depth, nodes_dev), BF16),
            pltpu.VMEM((SIDE, SIDE, share, depth), BF16),
            big,
            pltpu.VMEM((nblk, nblk), jnp.int32), pltpu.SMEM((nblk, nblk), jnp.int32),
            per_head, folded, folded, pltpu.VMEM((nodes, 256), BF16), folded, folded,
            pick, pick, blocks, blocks, blocks, blocks, turned, turned,
            pltpu.VMEM((BLK, nodes), F32),
            pltpu.VMEM((2, listed * BLK, 256), F32), pltpu.VMEM((1, nodes), F32),
            pltpu.VMEM((nblk // 4, listed * BLK, 256), BF16),
            pltpu.VMEM((BLK, nodes), BF16),
            pltpu.VMEM((nodes, 128), BF16),
            pltpu.VMEM((nblk * listed + 1, BLK, 128), BF16),
            pltpu.VMEM((nodes, 256), BF16),
            folded, per_head, folded, folded, per_head, folded,
            big,
            pltpu.VMEM((SIDE, share, depth), F32),
            half, half, pltpu.VMEM((SIDE, SIDE, share // 2, depth), F32), half,
            pltpu.VMEM((2, side, SIDE, rows, depth), BF16),
            pltpu.VMEM((2, SIDE, rows, depth), BF16),
            pltpu.VMEM((2, side, rows, depth), BF16),
            pltpu.VMEM((nz, share // 2, depth // nz), BF16),
            pltpu.VMEM((few, share // 2, depth // nz), BF16),
            pltpu.VMEM((2, nz, share // 2, depth // nz), BF16),
            pltpu.SemaphoreType.DMA((5,)), pltpu.SemaphoreType.DMA,
            dma(2, side), dma(2, side), dma(4, side), dma(seq - 1), dma(seq - 1), dma(seq - 1),
            dma(seq - 1), dma(seq - 1), dma(seq - 1), dma(SIDE), dma(SIDE + 1, side), dma(2, side),
            dma(few), dma(nz),
        ],
        compiler_params=pltpu.CompilerParams(
            collective_id=0, has_side_effects=True, vmem_limit_bytes=62 * 1024 * 1024),
        name="layer",
    )(cols, count, cols, count.reshape(1, nblk), order.reshape(nodes // 128, 128), q, k, v, g, wt)


def finish_kernel(*refs):
    arrays, outs, held, (load_sem, store_sem) = refs[:5], refs[5:10], refs[10:15], refs[15:]
    loads = [
        pltpu.make_async_copy(src, dst, load_sem.at[i])
        for i, (src, dst) in enumerate(zip(arrays, held))]
    stores = [
        pltpu.make_async_copy(src, dst, store_sem.at[i])
        for i, (src, dst) in enumerate(zip(held, outs))]
    for load in loads:
        load.start()
    for load, store in zip(loads, stores):
        load.wait()
        store.start()
    for store in stores:
        store.wait()


def finish(arrays):
    hbm = pl.BlockSpec(memory_space=pl.ANY)
    return pl.pallas_call(
        finish_kernel,
        out_shape=tuple(jax.ShapeDtypeStruct(a.shape, a.dtype) for a in arrays),
        in_specs=[hbm] * 5,
        out_specs=(hbm,) * 5,
        scratch_shapes=[pltpu.VMEM(a.shape, a.dtype) for a in arrays]
        + [pltpu.SemaphoreType.DMA((5,)), pltpu.SemaphoreType.DMA((5,))],
        compiler_params=pltpu.CompilerParams(vmem_limit_bytes=62 * 1024 * 1024),
        name="finish",
    )(*arrays)


def on_device(queries, key_vectors, value_vectors, out_grad, proj_weight,
              cluster_order, block_cols, block_count):
    seq, dps = lax.axis_size("seq"), lax.axis_size("dp")
    layer, dq, dk, dv, wg = finish(fused(
        queries[0], key_vectors[0], value_vectors[0], out_grad[0], proj_weight.T,
        cluster_order[0], block_cols[0].T, block_count[0], seq, dps))
    return layer[None], dq[None], dk[None], dv[None], wg.T


def solution(mesh):
    rows = P("dp", "seq", None)
    return jax.shard_map(
        on_device,
        mesh=mesh,
        in_specs=(rows, rows, rows, rows, P(None, "seq"),
                  P("dp", None), P("dp", None, None), P("dp", None)),
        out_specs=(rows, rows, rows, rows, P(None, "seq")),
        check_vma=False,
    )
```

```python
import jax
import jax.numpy as jnp
from jax import lax
from jax.experimental import pallas as pl
from jax.experimental.pallas import tpu as pltpu
from jax.sharding import PartitionSpec as P

MESH = pl.DeviceIdType.MESH
SIDE = 4
STEPS = (
    (2, 2), (3, 2), (2, 3), (1, 2), (2, 1), (2, 0), (0, 2), (3, 1), (1, 3), (3, 3), (1, 1),
    (3, 0), (1, 0), (0, 3), (0, 1))
TILE = 1024
BLK = 64
F32 = jnp.float32
BF16 = jnp.bfloat16
TRANS_B = (((1,), (1,)), ((), ()))


def push(src, dst, sems, at, device):
    copy = pltpu.make_async_remote_copy(
        src_ref=src, dst_ref=dst, send_sem=sems[0].at[at], recv_sem=sems[1].at[at],
        device_id=device, device_id_type=MESH)
    copy.start()
    return copy


def beside(a, b):
    return jnp.concatenate([a, b], axis=1)


def above(*parts):
    return jnp.concatenate(parts, axis=0)


def fused_kernel(
    cols_ref, count_ref, cols_vec, count_vec, order_ref, q_hbm, k_hbm, v_hbm, g_hbm, w_hbm,
    *rest,
):
    outs, (layer_ref, dq_ref, dk_ref, dv_ref, wg_ref) = rest[:5], rest[5:10]
    (
        q_ref, k_ref, v_ref, g_ref, gt_ref, wt_ref, up_ref, slots_vec, slots_ref,
        qk_out, v_out, b_out, x_ref, v_in, b_in,
        pick_ref, unpick_ref, qq_ref, kk_ref, vv_ref, bb_ref, kt_ref, vt_ref, bt_ref,
        score_ref, inv_ref, soft_ref, ot_ref, on_ref, term_ref, grads_ref,
        o_out, dkv_out, dq_out, o_in, dkv_in, dq_in,
        attn_ref, part_ref, mate_out, mate_in, sum_ref, half_ref, line_in, cross_out, cross_in,
        z_out, z_in, all_in,
        in_sem, out_sem, slot_sem, w1_sems, w2_sems, core_sems, qk_sems, v_sems, b_sems,
        o_sems, dkv_sems, dq_sems, mate_sems, line_sems, cross_sems, z_sems, all_sems,
    ) = rest[10:]
    dp, me = lax.axis_index("dp"), lax.axis_index("seq")
    seq, half_nodes, _ = v_out.shape
    nz = all_in.shape[1]
    nodes_dev = 2 * half_nodes
    nodes = seq * nodes_dev
    nblk = nodes // BLK
    listed = cols_ref.shape[0]
    chunks = listed // 4
    quads = nblk // 4
    depth = q_ref.shape[1]
    share = depth // seq
    y, x = me // SIDE, me % SIDE
    core, z = dp % 2, dp // 2
    mate = (dp + 1 - 2 * core, me)
    peers = [lax.rem(y + dy, SIDE) * SIDE + lax.rem(x + dx, SIDE) for dy, dx in STEPS]
    z_peers = [lax.rem(z + i, nz) for i in range(1, nz)]
    xs = [lax.rem(x + i, SIDE) for i in range(1, SIDE)]
    ys = [lax.rem(y + i, SIDE) for i in range(1, SIDE)]
    x_peers = [(dp, y * SIDE + at) for at in xs]
    y_peers = [(dp, at * SIDE + x) for at in ys]
    low128 = lax.broadcasted_iota(jnp.int32, (128, 128), 1) < BLK
    low = lax.broadcasted_iota(jnp.int32, (BLK, 128), 1) < BLK
    zero = jnp.zeros((BLK, 128), BF16)
    zero128 = jnp.zeros((128, 128), BF16)

    loads = [
        pltpu.make_async_copy(src, dst, in_sem.at[i])
        for i, (src, dst) in enumerate((
            (w_hbm, wt_ref.at[y, x]), (k_hbm, k_ref), (q_hbm, q_ref), (v_hbm, v_ref),
            (g_hbm, g_ref)))]
    for load in loads:
        load.start()
    results = (layer_ref, dq_ref, dk_ref, dv_ref, wg_ref)
    stores = [
        pltpu.make_async_copy(src, dst, out_sem.at[i])
        for i, (src, dst) in enumerate(zip(results, outs))]

    def store(i):
        stores[i].start()

    barrier = pltpu.get_barrier_semaphore()
    greeted = [(dp, p) for p in peers] + [(2 * p + core, me) for p in z_peers] + [mate]
    for device in greeted:
        pl.semaphore_signal(barrier, inc=1, device_id=device, device_id_type=MESH)
    pl.semaphore_wait(barrier, len(greeted))

    rows = share // 4
    start_a = pl.multiple_of(core * 2 * rows, 2 * rows)
    half_a = pl.ds(start_a, rows)
    half_b = pl.ds(pl.multiple_of(start_a + rows, rows), rows)
    loads[1].wait()
    loads[2].wait()
    for j in range(seq // 2):
        lanes = slice(128 * j, 128 * (j + 1))
        q, k = q_ref[:, lanes], k_ref[:, lanes]
        qk_out[2 * j] = beside(q[:, :BLK], k[:, :BLK])
        qk_out[2 * j + 1] = beside(q[:, BLK:], k[:, BLK:])
    own = pl.ds(pl.multiple_of(me * nodes_dev, nodes_dev), nodes_dev)
    x_ref[own, :128] = qk_out[me]
    qk_copies = [
        push(qk_out.at[p], x_ref.at[own, pl.ds(0, 128)], qk_sems, i, (dp, p))
        for i, p in enumerate(peers)]

    def fold(ref, out):
        for j in range(seq // 2):
            tile = ref[:, 128 * j:128 * (j + 1)]
            out[2 * j] = beside(tile[:half_nodes, :BLK], tile[half_nodes:, :BLK])
            out[2 * j + 1] = beside(tile[:half_nodes, BLK:], tile[half_nodes:, BLK:])

    def unfold(ref, out):
        for j in range(seq // 2):
            lanes = slice(128 * j, 128 * (j + 1))
            a, b = ref[2 * j], ref[2 * j + 1]
            out[:half_nodes, lanes] = beside(a[:, :BLK], b[:, :BLK])
            out[half_nodes:, lanes] = beside(a[:, BLK:], b[:, BLK:])

    loads[3].wait()
    fold(v_ref, v_out)
    v_in[me] = v_out[me]
    v_copies = [
        push(v_out.at[p], v_in.at[me], v_sems, i, (dp, p)) for i, p in enumerate(peers)]

    loads[0].wait()
    first, second, across = [], [], []
    for i in range(SIDE - 1):
        piece = wt_ref.at[y, x, half_a]
        first.append(push(piece, piece, w1_sems, (0, i), x_peers[i]))
        piece = wt_ref.at[y, x, half_b]
        first.append(push(piece, piece, w1_sems, (1, i), y_peers[i]))

    order = order_ref[...]
    order_col = jnp.transpose(
        above(order.astype(F32), jnp.zeros((128 - order.shape[0], 128), F32))).astype(jnp.int32)
    lane_node = lax.broadcasted_iota(jnp.int32, (128, nodes), 1)
    for i in range(nodes // 128):
        pick_ref[128 * i:128 * (i + 1), :] = (
            lane_node == order_col[:, i:i + 1]).astype(F32).astype(BF16)

    loads[4].wait()
    for i in range(depth // 128):
        gt_ref[128 * i:128 * (i + 1), :] = jnp.transpose(g_ref[:, 128 * i:128 * (i + 1)])
    order_row = jnp.concatenate([order[i:i + 1, :] for i in range(nodes // 128)], axis=1)
    row_node = lax.broadcasted_iota(jnp.int32, (128, nodes), 0)
    for j in range(nodes // 128):
        unpick_ref[128 * j:128 * (j + 1), :] = (
            row_node == order_row - 128 * j).astype(F32).astype(BF16)
    at_m = lax.broadcasted_iota(jnp.int32, (listed, nblk), 0)
    at_r = lax.broadcasted_iota(jnp.int32, (listed, nblk), 1)
    live_cols = jnp.where(at_m < count_vec[...], cols_vec[...], -1)
    place = at_r * listed + at_m
    for c in range(nblk):
        slots_vec[c:c + 1, :] = jnp.min(
            jnp.where(live_cols == c, place, nblk * listed), axis=0, keepdims=True)
    slot_copy = pltpu.make_async_copy(slots_vec, slots_ref, slot_sem)
    slot_copy.start()
    term_ref[nblk * listed] = zero

    for copy in qk_copies + v_copies:
        copy.wait_recv()
    for copy in first:
        copy.wait_recv()
    for i in range(SIDE - 1):
        piece = wt_ref.at[y, :, half_a]
        second.append(push(piece, piece, w2_sems, (0, i), y_peers[i]))
        piece = wt_ref.at[:, x, half_b]
        second.append(push(piece, piece, w2_sems, (1, i), x_peers[i]))
    for i in range(SIDE - 1):
        piece = wt_ref.at[y, xs[i], half_a]
        across.append(push(piece, piece, core_sems, (0, i), mate))
        piece = wt_ref.at[ys[i], x, half_b]
        across.append(push(piece, piece, core_sems, (1, i), mate))

    slot_copy.wait()
    empty = jnp.zeros((half_nodes, BLK), BF16)
    for s in range(seq):
        tile = v_in[s]
        x_ref[nodes_dev * s:nodes_dev * s + half_nodes, 128:] = beside(tile[:, :BLK], empty)
        x_ref[nodes_dev * s + half_nodes:nodes_dev * (s + 1), 128:] = beside(tile[:, BLK:], empty)

    def turned(ref, i, tile):
        swap = pltpu.roll(tile, BLK, 1).astype(BF16)
        tile = tile.astype(BF16)
        ref[0, 2 * i] = jnp.where(low, tile, zero)
        ref[1, 2 * i] = jnp.where(low, zero, swap)
        ref[0, 2 * i + 1] = jnp.where(low, swap, zero)
        ref[1, 2 * i + 1] = jnp.where(low, zero, tile)

    def twice(ref, i, tile):
        ref[2 * i] = tile[:BLK]
        ref[2 * i + 1] = tile[BLK:]

    def into_cluster(t, carry):
        here = pl.ds(pl.multiple_of(t * TILE, TILE), TILE)
        tile = jnp.dot(pick_ref[here, :], x_ref[...], preferred_element_type=F32)
        for k in range(TILE // 128):
            moved = tile[128 * k:128 * (k + 1)]
            i = t * (TILE // 128) + k
            qk, v = moved[:, :128], moved[:, 128:]
            kq = pltpu.roll(qk, BLK, 1)
            twice(qq_ref, i, (jnp.where(low128, qk, kq) * 0.125).astype(BF16))
            twice(kk_ref, i, jnp.where(low128, kq, qk).astype(BF16))
            twice(vv_ref, i, (v + pltpu.roll(v, BLK, 1)).astype(BF16))
            turned(kt_ref, i, jnp.transpose(qk)[BLK:])
            turned(vt_ref, i, jnp.transpose(v)[:BLK])
        return carry

    lax.fori_loop(0, nodes // TILE, into_cluster, 0)

    def diagonal(ref, i):
        blocks = []
        for j in range(4):
            tile = ref[4 * i + j]
            tile = jnp.where(low, tile, zero) if j % 2 == 0 else jnp.where(low, zero, tile)
            blocks.append(beside(tile, zero) if j < 2 else beside(zero, tile))
        return above(*blocks)

    def natural(ref, i, c):
        parts = []
        for m in range(4 * c, 4 * c + 4):
            a, b, d, e = (ref[cols_ref[m, 4 * i + j]] for j in range(4))
            parts.append(beside(jnp.where(low, a, b), jnp.where(low, d, e)))
        return above(*parts)

    def across_keys(ref, i, c):
        parts = []
        for j in range(4):
            r = 4 * i + j
            m = 4 * c
            parts.append(beside(
                ref[0, cols_ref[m, r]] + ref[1, cols_ref[m + 1, r]],
                ref[0, cols_ref[m + 2, r]] + ref[1, cols_ref[m + 3, r]]))
        return above(*parts)

    def diagonal_of(back):
        return beside(
            jnp.where(low, back[:BLK, :128], back[BLK:2 * BLK, :128]),
            jnp.where(low, back[2 * BLK:3 * BLK, 128:], back[3 * BLK:, 128:]))

    lane = lax.broadcasted_iota(jnp.int32, (1, 256), 1)

    def live_of(i):
        return jnp.where(
            lane < 2 * BLK,
            jnp.where(lane < BLK, count_ref[4 * i], count_ref[4 * i + 1]),
            jnp.where(lane < 3 * BLK, count_ref[4 * i + 2], count_ref[4 * i + 3]))

    def scores(i, c, weights, live, held, peak):
        score = lax.dot_general(
            natural(kk_ref, i, c), weights, TRANS_B, preferred_element_type=F32)
        for k in range(4):
            m = 4 * c + k
            part = jnp.where(m < live, score[k * BLK:(k + 1) * BLK], -jnp.inf)
            score_ref[held, m * BLK:(m + 1) * BLK, :] = part
            peak = jnp.maximum(peak, jnp.max(part.reshape(8, 8, 256), axis=0))
        return peak

    no_peak = jnp.full((8, 256), -jnp.inf, F32)

    def forward_step(i, held, peak):
        after = jnp.minimum(i + 1, quads - 1)
        weights, live = diagonal(qq_ref, after), live_of(after)
        peak = jnp.max(peak, axis=0, keepdims=True)
        total = jnp.zeros((8, 256), F32)
        back = jnp.zeros((256, 256), F32)
        next_peak = no_peak
        for c in range(chunks):
            next_peak = scores(after, c, weights, live, 1 - held, next_peak)
            here = slice(c * 256, (c + 1) * 256)
            terms = jnp.exp(score_ref[held, here, :] - peak)
            total = total + jnp.sum(terms.reshape(32, 8, 256), axis=0)
            terms = terms.astype(BF16)
            soft_ref[i, here, :] = terms
            back = back + jnp.dot(across_keys(vt_ref, i, c), terms, preferred_element_type=F32)
        inv = 1.0 / jnp.sum(total, axis=0, keepdims=True)
        there = pl.ds(pl.multiple_of(i * 256, 256), 256)
        inv_ref[:, there] = inv
        out = diagonal_of(back) * inv
        ot_ref[:, there] = out.astype(BF16)
        out = jnp.transpose(out).astype(BF16)
        on_ref[there, :] = beside(out, jnp.zeros_like(out))
        return next_peak

    def forward(i, peak):
        peak = forward_step(2 * i, 0, peak)
        return forward_step(2 * i + 1, 1, peak)

    def first_scores():
        peak = no_peak
        weights, live = diagonal(qq_ref, 0), live_of(0)
        for c in range(chunks):
            peak = scores(0, c, weights, live, 0, peak)
        return peak

    lax.fori_loop(0, quads // 2, forward, first_scores())

    for i in range(SIDE - 1):
        back = SIDE - 1 - i
        second[2 * i].wait_recv()
        piece = wt_ref.at[lax.rem(y + back, SIDE), :, half_a]
        across.append(push(piece, piece, core_sems, (2, i), mate))
        second[2 * i + 1].wait_recv()
        piece = wt_ref.at[:, lax.rem(x + back, SIDE), half_b]
        across.append(push(piece, piece, core_sems, (3, i), mate))
    def fold_rows(tile):
        return beside(tile[:half_nodes, :BLK], tile[half_nodes:, :BLK])

    def back_to_nodes(ref, lanes, out, pack):
        def step(t, carry):
            here = pl.ds(pl.multiple_of(t * TILE, TILE), TILE)
            tile = jnp.dot(
                unpick_ref[here, :], ref[:, lanes], preferred_element_type=F32).astype(BF16)
            for k in range(TILE // 128):
                out[t * (TILE // 128) + k] = pack(tile[128 * k:128 * (k + 1)])
            return carry

        lax.fori_loop(0, nodes // TILE, step, 0)

    back_to_nodes(on_ref, slice(0, 128), o_out, fold_rows)
    o_in[me] = o_out[me]
    o_copies = [
        push(o_out.at[p], o_in.at[me], o_sems, i, (dp, p)) for i, p in enumerate(peers)]

    for copy in across:
        copy.wait_recv()
    up_ref[...] = jnp.dot(
        g_ref[...], wt_ref[...].reshape(depth, depth), preferred_element_type=F32).astype(BF16)
    fold(up_ref, b_out)
    b_in[me] = b_out[me]
    b_copies = [
        push(b_out.at[p], b_in.at[me], b_sems, i, (dp, p)) for i, p in enumerate(peers)]

    for copy in o_copies:
        copy.wait_recv()
    unfold(o_in, attn_ref)
    keep = pl.ds(pl.multiple_of(core * (share // 2), share // 2), share // 2)
    give = pl.ds(pl.multiple_of((1 - core) * (share // 2), share // 2), share // 2)
    order_y = ys + [y]
    mate_copies = []
    for c, at in enumerate(order_y):
        there = pl.ds(pl.multiple_of(at * (SIDE * share), SIDE * share), SIDE * share)
        part_ref[...] = jnp.dot(
            gt_ref[there, :], attn_ref[...], preferred_element_type=F32).reshape(
                SIDE, share, depth)
        mate_out[at] = part_ref[:, give, :].astype(BF16)
        sum_ref[at] = part_ref[:, keep, :]
        mate_copies.append(push(mate_out.at[at], mate_in.at[at], mate_sems, c, mate))

    layer_ref[...] = lax.dot_general(
        attn_ref[...], wt_ref[...].reshape(depth, depth), TRANS_B,
        preferred_element_type=F32).astype(BF16)

    store(0)

    line_a, line_b = [], []
    for c, at in enumerate(order_y):
        mate_copies[c].wait_recv()
        total = sum_ref[at] + mate_in[at].astype(F32)
        sum_ref[at] = total
        half_ref[at] = total.astype(BF16)
        for i in range(SIDE - 1):
            line_a.append(push(
                half_ref.at[at, xs[i], pl.ds(0, rows)], line_in.at[0, i, at], line_sems, (c, i),
                x_peers[i]))
        if c < SIDE - 1:
            line_b.append(push(
                half_ref.at[at, :, pl.ds(rows, rows)], line_in.at[1, c], line_sems, (SIDE, c),
                y_peers[c]))
    for copy in b_copies:
        copy.wait_recv()
    for s in range(seq):
        tile = b_in[s]
        x_ref[nodes_dev * s:nodes_dev * s + half_nodes, 128:] = beside(
            tile[:, :BLK], tile[:, :BLK])
        x_ref[nodes_dev * s + half_nodes:nodes_dev * (s + 1), 128:] = beside(
            tile[:, BLK:], tile[:, BLK:])

    def upstream_into_cluster(t, carry):
        here = pl.ds(pl.multiple_of(t * TILE, TILE), TILE)
        tile = jnp.dot(pick_ref[here, :], x_ref[:, 128:], preferred_element_type=F32)
        for k in range(TILE // 128):
            moved = tile[128 * k:128 * (k + 1)]
            i = t * (TILE // 128) + k
            twice(bb_ref, i, moved.astype(BF16))
            bt_ref[:, pl.ds(pl.multiple_of(i * 128, 128), 128)] = jnp.transpose(moved)[:BLK]
        return carry

    lax.fori_loop(0, nodes // TILE, upstream_into_cluster, 0)

    def backward(i, carry):
        there = pl.ds(pl.multiple_of(i * 256, 256), 256)
        delta = jnp.sum(ot_ref[:, there].astype(F32) * bt_ref[:, there], axis=0, keepdims=True)
        weights = diagonal(bb_ref, i)
        pair_weights = []
        for j in (0, 2):
            q1, q2, b1, b2 = (ref[4 * i + j + k] for ref in (qq_ref, bb_ref) for k in (0, 1))
            pair_weights.append(above(
                beside(jnp.where(low, zero, b1), zero), beside(zero, jnp.where(low, zero, b2)),
                beside(jnp.where(low, q1, zero), zero), beside(zero, jnp.where(low, q2, zero))))
        inv = inv_ref[:, there]

        def grad_soft(c):
            return lax.dot_general(
                natural(vv_ref, i, c), weights, TRANS_B, preferred_element_type=F32)

        back = jnp.zeros((256, 256), F32)
        grad = grad_soft(0)
        for c in range(chunks):
            here = slice(c * 256, (c + 1) * 256)
            ahead = grad_soft(c + 1) if c + 1 < chunks else None
            soft = soft_ref[i, here, :].astype(F32) * inv
            grad = (soft * (grad - delta)).astype(BF16)
            soft = soft.astype(BF16)
            for j in range(2):
                lanes = slice(128 * j, 128 * (j + 1))
                terms = jnp.dot(
                    beside(soft[:, lanes], grad[:, lanes]), pair_weights[j],
                    preferred_element_type=F32).astype(BF16)
                for k in range(4):
                    m = 4 * c + k
                    slot = (4 * i + 2 * j) * listed + m
                    term_ref[slot] = terms[k * BLK:(k + 1) * BLK, :128]
                    term_ref[slot + listed] = terms[k * BLK:(k + 1) * BLK, 128:]
            back = back + jnp.dot(across_keys(kt_ref, i, c), grad, preferred_element_type=F32)
            grad = ahead
        grad_q = jnp.transpose(diagonal_of(back) * 0.125).astype(BF16)
        grads_ref[there, 128:] = beside(grad_q, jnp.zeros_like(grad_q))
        return carry

    def backward_pair(i, carry):
        return backward(2 * i + 1, backward(2 * i, carry))

    lax.fori_loop(0, quads // 2, backward_pair, 0)

    for copy in line_a + line_b:
        copy.wait_recv()
    sum_a = sum_ref[:, pl.ds(x, 1), :rows, :].reshape(SIDE, rows, depth)
    sum_b = sum_ref[pl.ds(y, 1), :, rows:, :].reshape(SIDE, rows, depth)
    for i in range(SIDE - 1):
        sum_a += line_in[0, i].astype(F32)
        sum_b += line_in[1, i].astype(F32)
    cross_out[0] = sum_a.astype(BF16)
    cross_out[1] = sum_b.astype(BF16)
    cross = []
    for i in range(SIDE - 1):
        cross.append(push(
            cross_out.at[0, ys[i]], cross_in.at[0, i], cross_sems, (0, i), y_peers[i]))
        cross.append(push(
            cross_out.at[1, xs[i]], cross_in.at[1, i], cross_sems, (1, i), x_peers[i]))

    def gather_terms(c, carry):
        total = jnp.zeros((BLK, 128), F32)
        for r in range(0, nblk, 2):
            pair = term_ref[slots_ref[c, r]] + term_ref[slots_ref[c, r + 1]]
            total = total + pair.astype(F32)
        grads_ref[pl.ds(pl.multiple_of(c * BLK, BLK), BLK), :128] = total.astype(BF16)
        return carry

    lax.fori_loop(0, nblk, gather_terms, 0)

    back_to_nodes(grads_ref, slice(0, 128), dkv_out, lambda tile: tile)
    dkv_in[me] = dkv_out[me]
    dkv_copies = [
        push(dkv_out.at[p], dkv_in.at[me], dkv_sems, i, (dp, p)) for i, p in enumerate(peers)]

    for copy in cross:
        copy.wait_recv()
    shard_a = cross_out[0, y].astype(F32)
    shard_b = cross_out[1, x].astype(F32)
    for i in range(SIDE - 1):
        shard_a += cross_in[0, i].astype(F32)
        shard_b += cross_in[1, i].astype(F32)
    shard = above(shard_a, shard_b)
    lanes = depth // nz
    for i in range(nz):
        z_out[i] = shard[:, i * lanes:(i + 1) * lanes].astype(BF16)
    z_copies = [
        push(z_out.at[p], z_in.at[i], z_sems, i, (2 * p + core, me))
        for i, p in enumerate(z_peers)]
    back_to_nodes(grads_ref, slice(128, 256), dq_out, fold_rows)
    dq_in[me] = dq_out[me]
    dq_copies = [
        push(dq_out.at[p], dq_in.at[me], dq_sems, i, (dp, p)) for i, p in enumerate(peers)]

    for copy in z_copies:
        copy.wait_recv()
    mine = z_out[z].astype(F32)
    for i in range(nz - 1):
        mine += z_in[i].astype(F32)
    all_in[core, z] = mine.astype(BF16)
    all_copies = [
        push(all_in.at[core, z], all_in.at[core, z], all_sems, i, (2 * p + core, me))
        for i, p in enumerate(z_peers)]

    for copy in dkv_copies:
        copy.wait_recv()
    for j in range(seq // 2):
        there = slice(128 * j, 128 * (j + 1))
        a, b = dkv_in[2 * j], dkv_in[2 * j + 1]
        dk_ref[:, there] = beside(a[:, :BLK], b[:, :BLK])
        dv_ref[:, there] = beside(a[:, BLK:], b[:, BLK:])
    store(2)
    store(3)
    for copy in dq_copies:
        copy.wait_recv()
    unfold(dq_in, dq_ref)
    store(1)
    for copy in all_copies:
        copy.wait_recv()
    all_copies.append(push(all_in.at[core], all_in.at[core], all_sems, nz - 1, mate))
    all_copies[-1].wait_recv()
    for c in range(2):
        for i in range(nz):
            wg_ref[c * (share // 2):(c + 1) * (share // 2), i * lanes:(i + 1) * lanes] = (
                all_in[c, i].astype(F32))
    store(4)
    for copy in (first + second + across + qk_copies + v_copies + b_copies + o_copies
                 + mate_copies + line_a + line_b + cross + z_copies + dkv_copies + dq_copies
                 + all_copies):
        copy.wait_send()
    for copy in stores:
        copy.wait()


def fused(q, k, v, g, wt, order, cols, count, seq, dps):
    nodes_dev, depth = q.shape
    nodes = seq * nodes_dev
    listed, nblk = cols.shape
    share = depth // seq
    nz = dps // 2
    rows = share // 4
    side = SIDE - 1
    smem = pl.BlockSpec(memory_space=pltpu.SMEM)
    vmem = pl.BlockSpec(memory_space=pltpu.VMEM)
    hbm = pl.BlockSpec(memory_space=pl.ANY)

    def dma(*shape):
        return (pltpu.SemaphoreType.DMA(shape), pltpu.SemaphoreType.DMA(shape))

    flat = jax.ShapeDtypeStruct((nodes_dev, depth), BF16)
    big = pltpu.VMEM((nodes_dev, depth), BF16)
    per_head = pltpu.VMEM((seq, nodes_dev, 128), BF16)
    folded = pltpu.VMEM((seq, nodes_dev // 2, 128), BF16)
    blocks = pltpu.VMEM((nblk, BLK, 128), BF16)
    turned = pltpu.VMEM((2, nblk, BLK, 128), BF16)
    pick = pltpu.VMEM((nodes, nodes), BF16)
    half = pltpu.VMEM((SIDE, SIDE, share // 2, depth), BF16)
    few = max(nz - 1, 1)
    return pl.pallas_call(
        fused_kernel,
        out_shape=(flat, flat, flat, flat, jax.ShapeDtypeStruct((share, depth), F32)),
        in_specs=[smem, smem, vmem, vmem, vmem] + [hbm] * 5,
        out_specs=(hbm,) * 5,
        scratch_shapes=[
            big, big, big, big, pltpu.VMEM((share, depth), F32),
            big, big, big, big, pltpu.VMEM((depth, nodes_dev), BF16),
            pltpu.VMEM((SIDE, SIDE, share, depth), BF16),
            big,
            pltpu.VMEM((nblk, nblk), jnp.int32), pltpu.SMEM((nblk, nblk), jnp.int32),
            per_head, folded, folded, pltpu.VMEM((nodes, 256), BF16), folded, folded,
            pick, pick, blocks, blocks, blocks, blocks, turned, turned,
            pltpu.VMEM((BLK, nodes), F32),
            pltpu.VMEM((2, listed * BLK, 256), F32), pltpu.VMEM((1, nodes), F32),
            pltpu.VMEM((nblk // 4, listed * BLK, 256), BF16),
            pltpu.VMEM((BLK, nodes), BF16),
            pltpu.VMEM((nodes, 128), BF16),
            pltpu.VMEM((nblk * listed + 1, BLK, 128), BF16),
            pltpu.VMEM((nodes, 256), BF16),
            folded, per_head, folded, folded, per_head, folded,
            big,
            pltpu.VMEM((SIDE, share, depth), F32),
            half, half, pltpu.VMEM((SIDE, SIDE, share // 2, depth), F32), half,
            pltpu.VMEM((2, side, SIDE, rows, depth), BF16),
            pltpu.VMEM((2, SIDE, rows, depth), BF16),
            pltpu.VMEM((2, side, rows, depth), BF16),
            pltpu.VMEM((nz, share // 2, depth // nz), BF16),
            pltpu.VMEM((few, share // 2, depth // nz), BF16),
            pltpu.VMEM((2, nz, share // 2, depth // nz), BF16),
            pltpu.SemaphoreType.DMA((5,)), pltpu.SemaphoreType.DMA((5,)), pltpu.SemaphoreType.DMA,
            dma(2, side), dma(2, side), dma(4, side), dma(seq - 1), dma(seq - 1), dma(seq - 1),
            dma(seq - 1), dma(seq - 1), dma(seq - 1), dma(SIDE), dma(SIDE + 1, side), dma(2, side),
            dma(few), dma(nz),
        ],
        compiler_params=pltpu.CompilerParams(
            collective_id=0, has_side_effects=True, vmem_limit_bytes=62 * 1024 * 1024),
        name="layer",
    )(cols, count, cols, count.reshape(1, nblk), order.reshape(nodes // 128, 128), q, k, v, g, wt)


def finish_kernel(*refs):
    arrays, outs, held, (load_sem, store_sem) = refs[:5], refs[5:10], refs[10:15], refs[15:]
    loads = [
        pltpu.make_async_copy(src, dst, load_sem.at[i])
        for i, (src, dst) in enumerate(zip(arrays, held))]
    stores = [
        pltpu.make_async_copy(src, dst, store_sem.at[i])
        for i, (src, dst) in enumerate(zip(held, outs))]
    for load in loads:
        load.start()
    for load, store in zip(loads, stores):
        load.wait()
        store.start()
    for store in stores:
        store.wait()


def finish(arrays):
    hbm = pl.BlockSpec(memory_space=pl.ANY)
    return pl.pallas_call(
        finish_kernel,
        out_shape=tuple(jax.ShapeDtypeStruct(a.shape, a.dtype) for a in arrays),
        in_specs=[hbm] * 5,
        out_specs=(hbm,) * 5,
        scratch_shapes=[pltpu.VMEM(a.shape, a.dtype) for a in arrays]
        + [pltpu.SemaphoreType.DMA((5,)), pltpu.SemaphoreType.DMA((5,))],
        compiler_params=pltpu.CompilerParams(vmem_limit_bytes=62 * 1024 * 1024),
        name="finish",
    )(*arrays)


def on_device(queries, key_vectors, value_vectors, out_grad, proj_weight,
              cluster_order, block_cols, block_count):
    seq, dps = lax.axis_size("seq"), lax.axis_size("dp")
    layer, dq, dk, dv, wg = finish(fused(
        queries[0], key_vectors[0], value_vectors[0], out_grad[0], proj_weight.T,
        cluster_order[0], block_cols[0].T, block_count[0], seq, dps))
    return layer[None], dq[None], dk[None], dv[None], wg.T


def solution(mesh):
    rows = P("dp", "seq", None)
    return jax.shard_map(
        on_device,
        mesh=mesh,
        in_specs=(rows, rows, rows, rows, P(None, "seq"),
                  P("dp", None), P("dp", None, None), P("dp", None)),
        out_specs=(rows, rows, rows, rows, P(None, "seq")),
        check_vma=False,
    )
```

```python
import jax
import jax.numpy as jnp
from jax import lax
from jax.experimental import pallas as pl
from jax.experimental.pallas import tpu as pltpu
from jax.sharding import PartitionSpec as P

MESH = pl.DeviceIdType.MESH
SIDE = 4
STEPS = (
    (2, 2), (3, 2), (2, 3), (1, 2), (2, 1), (2, 0), (0, 2), (3, 1), (1, 3), (3, 3), (1, 1),
    (3, 0), (1, 0), (0, 3), (0, 1))
TILE = 1024
BLK = 64
F32 = jnp.float32
BF16 = jnp.bfloat16
TRANS_B = (((1,), (1,)), ((), ()))


def push(src, dst, sems, at, device):
    copy = pltpu.make_async_remote_copy(
        src_ref=src, dst_ref=dst, send_sem=sems[0].at[at], recv_sem=sems[1].at[at],
        device_id=device, device_id_type=MESH)
    copy.start()
    return copy


def beside(a, b):
    return jnp.concatenate([a, b], axis=1)


def above(*parts):
    return jnp.concatenate(parts, axis=0)


def fused_kernel(
    cols_ref, count_ref, cols_vec, count_vec, order_ref, q_hbm, k_hbm, v_hbm, g_hbm, w_hbm,
    *rest,
):
    outs, (layer_ref, dq_ref, dk_ref, dv_ref, wg_ref) = rest[:5], rest[5:10]
    (
        q_ref, k_ref, v_ref, g_ref, gt_ref, wt_ref, up_ref, slots_vec, slots_ref,
        qk_out, v_out, b_out, x_ref, v_in, b_in,
        pick_ref, unpick_ref, qq_ref, kk_ref, vv_ref, bb_ref, kt_ref, vt_ref, bt_ref,
        score_ref, inv_ref, soft_ref, ot_ref, on_ref, term_ref, grads_ref,
        o_out, dkv_out, dq_out, o_in, dkv_in, dq_in,
        attn_ref, part_ref, mate_out, mate_in, sum_ref, half_ref, line_in, cross_out, cross_in,
        z_out, z_in, all_in,
        in_sem, out_sem, slot_sem, w1_sems, w2_sems, core_sems, qk_sems, v_sems, b_sems,
        o_sems, dkv_sems, dq_sems, mate_sems, line_sems, cross_sems, z_sems, all_sems,
    ) = rest[10:]
    dp, me = lax.axis_index("dp"), lax.axis_index("seq")
    seq, half_nodes, _ = v_out.shape
    nz = all_in.shape[1]
    nodes_dev = 2 * half_nodes
    nodes = seq * nodes_dev
    nblk = nodes // BLK
    listed = cols_ref.shape[0]
    chunks = listed // 4
    quads = nblk // 4
    depth = q_ref.shape[1]
    share = depth // seq
    y, x = me // SIDE, me % SIDE
    core, z = dp % 2, dp // 2
    mate = (dp + 1 - 2 * core, me)
    peers = [lax.rem(y + dy, SIDE) * SIDE + lax.rem(x + dx, SIDE) for dy, dx in STEPS]
    z_peers = [lax.rem(z + i, nz) for i in range(1, nz)]
    xs = [lax.rem(x + i, SIDE) for i in range(1, SIDE)]
    ys = [lax.rem(y + i, SIDE) for i in range(1, SIDE)]
    x_peers = [(dp, y * SIDE + at) for at in xs]
    y_peers = [(dp, at * SIDE + x) for at in ys]
    low128 = lax.broadcasted_iota(jnp.int32, (128, 128), 1) < BLK
    low = lax.broadcasted_iota(jnp.int32, (BLK, 128), 1) < BLK
    zero = jnp.zeros((BLK, 128), BF16)
    zero128 = jnp.zeros((128, 128), BF16)

    loads = [
        pltpu.make_async_copy(src, dst, in_sem.at[i])
        for i, (src, dst) in enumerate((
            (w_hbm, wt_ref.at[y, x]), (k_hbm, k_ref), (q_hbm, q_ref), (v_hbm, v_ref),
            (g_hbm, g_ref)))]
    for load in loads:
        load.start()
    results = (layer_ref, dq_ref, dk_ref, dv_ref, wg_ref)
    stores = [
        pltpu.make_async_copy(src, dst, out_sem.at[i])
        for i, (src, dst) in enumerate(zip(results, outs))]

    def store(i):
        stores[i].start()

    barrier = pltpu.get_barrier_semaphore()
    greeted = [(dp, p) for p in peers] + [(2 * p + core, me) for p in z_peers] + [mate]
    for device in greeted:
        pl.semaphore_signal(barrier, inc=1, device_id=device, device_id_type=MESH)
    pl.semaphore_wait(barrier, len(greeted))

    rows = share // 4
    start_a = pl.multiple_of(core * 2 * rows, 2 * rows)
    half_a = pl.ds(start_a, rows)
    half_b = pl.ds(pl.multiple_of(start_a + rows, rows), rows)
    loads[1].wait()
    loads[2].wait()
    for j in range(seq // 2):
        lanes = slice(128 * j, 128 * (j + 1))
        q, k = q_ref[:, lanes], k_ref[:, lanes]
        qk_out[2 * j] = beside(q[:, :BLK], k[:, :BLK])
        qk_out[2 * j + 1] = beside(q[:, BLK:], k[:, BLK:])
    own = pl.ds(pl.multiple_of(me * nodes_dev, nodes_dev), nodes_dev)
    x_ref[own, :128] = qk_out[me]
    qk_copies = [
        push(qk_out.at[p], x_ref.at[own, pl.ds(0, 128)], qk_sems, i, (dp, p))
        for i, p in enumerate(peers)]

    def fold(ref, out):
        for j in range(seq // 2):
            tile = ref[:, 128 * j:128 * (j + 1)]
            out[2 * j] = beside(tile[:half_nodes, :BLK], tile[half_nodes:, :BLK])
            out[2 * j + 1] = beside(tile[:half_nodes, BLK:], tile[half_nodes:, BLK:])

    def unfold(ref, out):
        for j in range(seq // 2):
            lanes = slice(128 * j, 128 * (j + 1))
            a, b = ref[2 * j], ref[2 * j + 1]
            out[:half_nodes, lanes] = beside(a[:, :BLK], b[:, :BLK])
            out[half_nodes:, lanes] = beside(a[:, BLK:], b[:, BLK:])

    loads[3].wait()
    fold(v_ref, v_out)
    v_in[me] = v_out[me]
    v_copies = [
        push(v_out.at[p], v_in.at[me], v_sems, i, (dp, p)) for i, p in enumerate(peers)]

    loads[0].wait()
    first, second, across = [], [], []
    for i in range(SIDE - 1):
        piece = wt_ref.at[y, x, half_a]
        first.append(push(piece, piece, w1_sems, (0, i), x_peers[i]))
        piece = wt_ref.at[y, x, half_b]
        first.append(push(piece, piece, w1_sems, (1, i), y_peers[i]))

    order = order_ref[...]
    order_col = jnp.transpose(
        above(order.astype(F32), jnp.zeros((128 - order.shape[0], 128), F32))).astype(jnp.int32)
    lane_node = lax.broadcasted_iota(jnp.int32, (128, nodes), 1)
    for i in range(nodes // 128):
        pick_ref[128 * i:128 * (i + 1), :] = (
            lane_node == order_col[:, i:i + 1]).astype(F32).astype(BF16)

    loads[4].wait()
    for i in range(depth // 128):
        gt_ref[128 * i:128 * (i + 1), :] = jnp.transpose(g_ref[:, 128 * i:128 * (i + 1)])
    order_row = jnp.concatenate([order[i:i + 1, :] for i in range(nodes // 128)], axis=1)
    row_node = lax.broadcasted_iota(jnp.int32, (128, nodes), 0)
    for j in range(nodes // 128):
        unpick_ref[128 * j:128 * (j + 1), :] = (
            row_node == order_row - 128 * j).astype(F32).astype(BF16)
    at_m = lax.broadcasted_iota(jnp.int32, (listed, nblk), 0)
    at_r = lax.broadcasted_iota(jnp.int32, (listed, nblk), 1)
    live_cols = jnp.where(at_m < count_vec[...], cols_vec[...], -1)
    place = at_r * listed + at_m
    for c in range(nblk):
        slots_vec[c:c + 1, :] = jnp.min(
            jnp.where(live_cols == c, place, nblk * listed), axis=0, keepdims=True)
    slot_copy = pltpu.make_async_copy(slots_vec, slots_ref, slot_sem)
    slot_copy.start()
    term_ref[nblk * listed] = zero

    for copy in qk_copies:
        copy.wait_recv()
    slot_copy.wait()

    def turned(ref, i, tile):
        swap = pltpu.roll(tile, BLK, 1).astype(BF16)
        tile = tile.astype(BF16)
        ref[0, 2 * i] = jnp.where(low, tile, zero)
        ref[1, 2 * i] = jnp.where(low, zero, swap)
        ref[0, 2 * i + 1] = jnp.where(low, swap, zero)
        ref[1, 2 * i + 1] = jnp.where(low, zero, tile)

    def twice(ref, i, tile):
        ref[2 * i] = tile[:BLK]
        ref[2 * i + 1] = tile[BLK:]

    def keys_into_cluster(t, carry):
        here = pl.ds(pl.multiple_of(t * TILE, TILE), TILE)
        tile = jnp.dot(pick_ref[here, :], x_ref[:, :128], preferred_element_type=F32)
        for k in range(TILE // 128):
            qk = tile[128 * k:128 * (k + 1)]
            i = t * (TILE // 128) + k
            kq = pltpu.roll(qk, BLK, 1)
            twice(qq_ref, i, (jnp.where(low128, qk, kq) * 0.125).astype(BF16))
            twice(kk_ref, i, jnp.where(low128, kq, qk).astype(BF16))
            turned(kt_ref, i, jnp.transpose(qk)[BLK:])
        return carry

    lax.fori_loop(0, nodes // TILE, keys_into_cluster, 0)

    for copy in v_copies:
        copy.wait_recv()
    for copy in first:
        copy.wait_recv()
    for i in range(SIDE - 1):
        piece = wt_ref.at[y, :, half_a]
        second.append(push(piece, piece, w2_sems, (0, i), y_peers[i]))
        piece = wt_ref.at[:, x, half_b]
        second.append(push(piece, piece, w2_sems, (1, i), x_peers[i]))
    for i in range(SIDE - 1):
        piece = wt_ref.at[y, xs[i], half_a]
        across.append(push(piece, piece, core_sems, (0, i), mate))
        piece = wt_ref.at[ys[i], x, half_b]
        across.append(push(piece, piece, core_sems, (1, i), mate))

    empty = jnp.zeros((half_nodes, BLK), BF16)
    for s in range(seq):
        tile = v_in[s]
        x_ref[nodes_dev * s:nodes_dev * s + half_nodes, 128:] = beside(tile[:, :BLK], empty)
        x_ref[nodes_dev * s + half_nodes:nodes_dev * (s + 1), 128:] = beside(tile[:, BLK:], empty)

    def values_into_cluster(t, carry):
        here = pl.ds(pl.multiple_of(t * TILE, TILE), TILE)
        tile = jnp.dot(pick_ref[here, :], x_ref[:, 128:], preferred_element_type=F32)
        for k in range(TILE // 128):
            v = tile[128 * k:128 * (k + 1)]
            i = t * (TILE // 128) + k
            twice(vv_ref, i, (v + pltpu.roll(v, BLK, 1)).astype(BF16))
            turned(vt_ref, i, jnp.transpose(v)[:BLK])
        return carry

    lax.fori_loop(0, nodes // TILE, values_into_cluster, 0)

    def diagonal(ref, i):
        blocks = []
        for j in range(4):
            tile = ref[4 * i + j]
            tile = jnp.where(low, tile, zero) if j % 2 == 0 else jnp.where(low, zero, tile)
            blocks.append(beside(tile, zero) if j < 2 else beside(zero, tile))
        return above(*blocks)

    def natural(ref, i, c):
        parts = []
        for m in range(4 * c, 4 * c + 4):
            a, b, d, e = (ref[cols_ref[m, 4 * i + j]] for j in range(4))
            parts.append(beside(jnp.where(low, a, b), jnp.where(low, d, e)))
        return above(*parts)

    def across_keys(ref, i, c):
        parts = []
        for j in range(4):
            r = 4 * i + j
            m = 4 * c
            parts.append(beside(
                ref[0, cols_ref[m, r]] + ref[1, cols_ref[m + 1, r]],
                ref[0, cols_ref[m + 2, r]] + ref[1, cols_ref[m + 3, r]]))
        return above(*parts)

    def diagonal_of(back):
        return beside(
            jnp.where(low, back[:BLK, :128], back[BLK:2 * BLK, :128]),
            jnp.where(low, back[2 * BLK:3 * BLK, 128:], back[3 * BLK:, 128:]))

    lane = lax.broadcasted_iota(jnp.int32, (1, 256), 1)

    def live_of(i):
        return jnp.where(
            lane < 2 * BLK,
            jnp.where(lane < BLK, count_ref[4 * i], count_ref[4 * i + 1]),
            jnp.where(lane < 3 * BLK, count_ref[4 * i + 2], count_ref[4 * i + 3]))

    def scores(i, c, weights, live, held, peak):
        score = lax.dot_general(
            natural(kk_ref, i, c), weights, TRANS_B, preferred_element_type=F32)
        for k in range(4):
            m = 4 * c + k
            part = jnp.where(m < live, score[k * BLK:(k + 1) * BLK], -jnp.inf)
            score_ref[held, m * BLK:(m + 1) * BLK, :] = part
            peak = jnp.maximum(peak, jnp.max(part.reshape(8, 8, 256), axis=0))
        return peak

    no_peak = jnp.full((8, 256), -jnp.inf, F32)

    def forward_step(i, held, peak):
        after = jnp.minimum(i + 1, quads - 1)
        weights, live = diagonal(qq_ref, after), live_of(after)
        peak = jnp.max(peak, axis=0, keepdims=True)
        total = jnp.zeros((8, 256), F32)
        back = jnp.zeros((256, 256), F32)
        next_peak = no_peak
        for c in range(chunks):
            next_peak = scores(after, c, weights, live, 1 - held, next_peak)
            here = slice(c * 256, (c + 1) * 256)
            terms = jnp.exp(score_ref[held, here, :] - peak)
            total = total + jnp.sum(terms.reshape(32, 8, 256), axis=0)
            terms = terms.astype(BF16)
            soft_ref[i, here, :] = terms
            back = back + jnp.dot(across_keys(vt_ref, i, c), terms, preferred_element_type=F32)
        inv = 1.0 / jnp.sum(total, axis=0, keepdims=True)
        there = pl.ds(pl.multiple_of(i * 256, 256), 256)
        inv_ref[:, there] = inv
        out = diagonal_of(back) * inv
        ot_ref[:, there] = out.astype(BF16)
        out = jnp.transpose(out).astype(BF16)
        on_ref[there, :] = beside(out, jnp.zeros_like(out))
        return next_peak

    def forward(i, peak):
        peak = forward_step(2 * i, 0, peak)
        return forward_step(2 * i + 1, 1, peak)

    def first_scores():
        peak = no_peak
        weights, live = diagonal(qq_ref, 0), live_of(0)
        for c in range(chunks):
            peak = scores(0, c, weights, live, 0, peak)
        return peak

    lax.fori_loop(0, quads // 2, forward, first_scores())

    for i in range(SIDE - 1):
        back = SIDE - 1 - i
        second[2 * i].wait_recv()
        piece = wt_ref.at[lax.rem(y + back, SIDE), :, half_a]
        across.append(push(piece, piece, core_sems, (2, i), mate))
        second[2 * i + 1].wait_recv()
        piece = wt_ref.at[:, lax.rem(x + back, SIDE), half_b]
        across.append(push(piece, piece, core_sems, (3, i), mate))
    def fold_rows(tile):
        return beside(tile[:half_nodes, :BLK], tile[half_nodes:, :BLK])

    def back_to_nodes(ref, lanes, out, pack):
        def step(t, carry):
            here = pl.ds(pl.multiple_of(t * TILE, TILE), TILE)
            tile = jnp.dot(
                unpick_ref[here, :], ref[:, lanes], preferred_element_type=F32).astype(BF16)
            for k in range(TILE // 128):
                out[t * (TILE // 128) + k] = pack(tile[128 * k:128 * (k + 1)])
            return carry

        lax.fori_loop(0, nodes // TILE, step, 0)

    back_to_nodes(on_ref, slice(0, 128), o_out, fold_rows)
    o_in[me] = o_out[me]
    o_copies = [
        push(o_out.at[p], o_in.at[me], o_sems, i, (dp, p)) for i, p in enumerate(peers)]

    for copy in across:
        copy.wait_recv()
    up_ref[...] = jnp.dot(
        g_ref[...], wt_ref[...].reshape(depth, depth), preferred_element_type=F32).astype(BF16)
    fold(up_ref, b_out)
    b_in[me] = b_out[me]
    b_copies = [
        push(b_out.at[p], b_in.at[me], b_sems, i, (dp, p)) for i, p in enumerate(peers)]

    for copy in o_copies:
        copy.wait_recv()
    unfold(o_in, attn_ref)
    keep = pl.ds(pl.multiple_of(core * (share // 2), share // 2), share // 2)
    give = pl.ds(pl.multiple_of((1 - core) * (share // 2), share // 2), share // 2)
    order_y = ys + [y]
    mate_copies = []
    for c, at in enumerate(order_y):
        there = pl.ds(pl.multiple_of(at * (SIDE * share), SIDE * share), SIDE * share)
        part_ref[...] = jnp.dot(
            gt_ref[there, :], attn_ref[...], preferred_element_type=F32).reshape(
                SIDE, share, depth)
        mate_out[at] = part_ref[:, give, :].astype(BF16)
        sum_ref[at] = part_ref[:, keep, :]
        mate_copies.append(push(mate_out.at[at], mate_in.at[at], mate_sems, c, mate))

    line_a, line_b = [], []
    for c, at in enumerate(order_y):
        mate_copies[c].wait_recv()
        total = sum_ref[at] + mate_in[at].astype(F32)
        sum_ref[at] = total
        half_ref[at] = total.astype(BF16)
        for i in range(SIDE - 1):
            line_a.append(push(
                half_ref.at[at, xs[i], pl.ds(0, rows)], line_in.at[0, i, at], line_sems, (c, i),
                x_peers[i]))
        if c < SIDE - 1:
            line_b.append(push(
                half_ref.at[at, :, pl.ds(rows, rows)], line_in.at[1, c], line_sems, (SIDE, c),
                y_peers[c]))
    layer_ref[...] = lax.dot_general(
        attn_ref[...], wt_ref[...].reshape(depth, depth), TRANS_B,
        preferred_element_type=F32).astype(BF16)

    store(0)

    for copy in b_copies:
        copy.wait_recv()
    for s in range(seq):
        tile = b_in[s]
        x_ref[nodes_dev * s:nodes_dev * s + half_nodes, 128:] = beside(
            tile[:, :BLK], tile[:, :BLK])
        x_ref[nodes_dev * s + half_nodes:nodes_dev * (s + 1), 128:] = beside(
            tile[:, BLK:], tile[:, BLK:])

    def upstream_into_cluster(t, carry):
        here = pl.ds(pl.multiple_of(t * TILE, TILE), TILE)
        tile = jnp.dot(pick_ref[here, :], x_ref[:, 128:], preferred_element_type=F32)
        for k in range(TILE // 128):
            moved = tile[128 * k:128 * (k + 1)]
            i = t * (TILE // 128) + k
            twice(bb_ref, i, moved.astype(BF16))
            bt_ref[:, pl.ds(pl.multiple_of(i * 128, 128), 128)] = jnp.transpose(moved)[:BLK]
        return carry

    lax.fori_loop(0, nodes // TILE, upstream_into_cluster, 0)

    def backward(i, carry):
        there = pl.ds(pl.multiple_of(i * 256, 256), 256)
        delta = jnp.sum(ot_ref[:, there].astype(F32) * bt_ref[:, there], axis=0, keepdims=True)
        weights = diagonal(bb_ref, i)
        pair_weights = []
        for j in (0, 2):
            q1, q2, b1, b2 = (ref[4 * i + j + k] for ref in (qq_ref, bb_ref) for k in (0, 1))
            pair_weights.append(above(
                beside(jnp.where(low, zero, b1), zero), beside(zero, jnp.where(low, zero, b2)),
                beside(jnp.where(low, q1, zero), zero), beside(zero, jnp.where(low, q2, zero))))
        inv = inv_ref[:, there]

        def grad_soft(c):
            return lax.dot_general(
                natural(vv_ref, i, c), weights, TRANS_B, preferred_element_type=F32)

        back = jnp.zeros((256, 256), F32)
        grad = grad_soft(0)
        for c in range(chunks):
            here = slice(c * 256, (c + 1) * 256)
            ahead = grad_soft(c + 1) if c + 1 < chunks else None
            soft = soft_ref[i, here, :].astype(F32) * inv
            grad = (soft * (grad - delta)).astype(BF16)
            soft = soft.astype(BF16)
            for j in range(2):
                lanes = slice(128 * j, 128 * (j + 1))
                terms = jnp.dot(
                    beside(soft[:, lanes], grad[:, lanes]), pair_weights[j],
                    preferred_element_type=F32).astype(BF16)
                for k in range(4):
                    m = 4 * c + k
                    slot = (4 * i + 2 * j) * listed + m
                    term_ref[slot] = terms[k * BLK:(k + 1) * BLK, :128]
                    term_ref[slot + listed] = terms[k * BLK:(k + 1) * BLK, 128:]
            back = back + jnp.dot(across_keys(kt_ref, i, c), grad, preferred_element_type=F32)
            grad = ahead
        grad_q = jnp.transpose(diagonal_of(back) * 0.125).astype(BF16)
        grads_ref[there, 128:] = beside(grad_q, jnp.zeros_like(grad_q))
        return carry

    def backward_pair(i, carry):
        return backward(2 * i + 1, backward(2 * i, carry))

    lax.fori_loop(0, quads // 2, backward_pair, 0)

    for copy in line_a + line_b:
        copy.wait_recv()
    sum_a = sum_ref[:, pl.ds(x, 1), :rows, :].reshape(SIDE, rows, depth)
    sum_b = sum_ref[pl.ds(y, 1), :, rows:, :].reshape(SIDE, rows, depth)
    for i in range(SIDE - 1):
        sum_a += line_in[0, i].astype(F32)
        sum_b += line_in[1, i].astype(F32)
    cross_out[0] = sum_a.astype(BF16)
    cross_out[1] = sum_b.astype(BF16)
    cross = []
    for i in range(SIDE - 1):
        cross.append(push(
            cross_out.at[0, ys[i]], cross_in.at[0, i], cross_sems, (0, i), y_peers[i]))
        cross.append(push(
            cross_out.at[1, xs[i]], cross_in.at[1, i], cross_sems, (1, i), x_peers[i]))

    def gather_terms(c, carry):
        total = jnp.zeros((BLK, 128), F32)
        for r in range(0, nblk, 2):
            pair = term_ref[slots_ref[c, r]] + term_ref[slots_ref[c, r + 1]]
            total = total + pair.astype(F32)
        grads_ref[pl.ds(pl.multiple_of(c * BLK, BLK), BLK), :128] = total.astype(BF16)
        return carry

    lax.fori_loop(0, nblk, gather_terms, 0)

    back_to_nodes(grads_ref, slice(0, 128), dkv_out, lambda tile: tile)
    dkv_in[me] = dkv_out[me]
    dkv_copies = [
        push(dkv_out.at[p], dkv_in.at[me], dkv_sems, i, (dp, p)) for i, p in enumerate(peers)]

    for copy in cross:
        copy.wait_recv()
    shard_a = cross_out[0, y].astype(F32)
    shard_b = cross_out[1, x].astype(F32)
    for i in range(SIDE - 1):
        shard_a += cross_in[0, i].astype(F32)
        shard_b += cross_in[1, i].astype(F32)
    shard = above(shard_a, shard_b)
    lanes = depth // nz
    for i in range(nz):
        z_out[i] = shard[:, i * lanes:(i + 1) * lanes].astype(BF16)
    z_copies = [
        push(z_out.at[p], z_in.at[i], z_sems, i, (2 * p + core, me))
        for i, p in enumerate(z_peers)]
    back_to_nodes(grads_ref, slice(128, 256), dq_out, fold_rows)
    dq_in[me] = dq_out[me]
    dq_copies = [
        push(dq_out.at[p], dq_in.at[me], dq_sems, i, (dp, p)) for i, p in enumerate(peers)]

    for copy in z_copies:
        copy.wait_recv()
    mine = z_out[z].astype(F32)
    for i in range(nz - 1):
        mine += z_in[i].astype(F32)
    all_in[core, z] = mine.astype(BF16)
    all_copies = [
        push(all_in.at[core, z], all_in.at[core, z], all_sems, i, (2 * p + core, me))
        for i, p in enumerate(z_peers)]

    for copy in dkv_copies:
        copy.wait_recv()
    for j in range(seq // 2):
        there = slice(128 * j, 128 * (j + 1))
        a, b = dkv_in[2 * j], dkv_in[2 * j + 1]
        dk_ref[:, there] = beside(a[:, :BLK], b[:, :BLK])
        dv_ref[:, there] = beside(a[:, BLK:], b[:, BLK:])
    store(2)
    store(3)
    for copy in dq_copies:
        copy.wait_recv()
    unfold(dq_in, dq_ref)
    store(1)
    for copy in all_copies:
        copy.wait_recv()
    all_copies.append(push(all_in.at[core], all_in.at[core], all_sems, nz - 1, mate))
    all_copies[-1].wait_recv()
    for c in range(2):
        for i in range(nz):
            wg_ref[c * (share // 2):(c + 1) * (share // 2), i * lanes:(i + 1) * lanes] = (
                all_in[c, i].astype(F32))
    store(4)
    for copy in (first + second + across + qk_copies + v_copies + b_copies + o_copies
                 + mate_copies + line_a + line_b + cross + z_copies + dkv_copies + dq_copies
                 + all_copies):
        copy.wait_send()
    for copy in stores:
        copy.wait()


def fused(q, k, v, g, wt, order, cols, count, seq, dps):
    nodes_dev, depth = q.shape
    nodes = seq * nodes_dev
    listed, nblk = cols.shape
    share = depth // seq
    nz = dps // 2
    rows = share // 4
    side = SIDE - 1
    smem = pl.BlockSpec(memory_space=pltpu.SMEM)
    vmem = pl.BlockSpec(memory_space=pltpu.VMEM)
    hbm = pl.BlockSpec(memory_space=pl.ANY)

    def dma(*shape):
        return (pltpu.SemaphoreType.DMA(shape), pltpu.SemaphoreType.DMA(shape))

    flat = jax.ShapeDtypeStruct((nodes_dev, depth), BF16)
    big = pltpu.VMEM((nodes_dev, depth), BF16)
    per_head = pltpu.VMEM((seq, nodes_dev, 128), BF16)
    folded = pltpu.VMEM((seq, nodes_dev // 2, 128), BF16)
    blocks = pltpu.VMEM((nblk, BLK, 128), BF16)
    turned = pltpu.VMEM((2, nblk, BLK, 128), BF16)
    pick = pltpu.VMEM((nodes, nodes), BF16)
    half = pltpu.VMEM((SIDE, SIDE, share // 2, depth), BF16)
    few = max(nz - 1, 1)
    return pl.pallas_call(
        fused_kernel,
        out_shape=(flat, flat, flat, flat, jax.ShapeDtypeStruct((share, depth), F32)),
        in_specs=[smem, smem, vmem, vmem, vmem] + [hbm] * 5,
        out_specs=(hbm,) * 5,
        scratch_shapes=[
            big, big, big, big, pltpu.VMEM((share, depth), F32),
            big, big, big, big, pltpu.VMEM((depth, nodes_dev), BF16),
            pltpu.VMEM((SIDE, SIDE, share, depth), BF16),
            big,
            pltpu.VMEM((nblk, nblk), jnp.int32), pltpu.SMEM((nblk, nblk), jnp.int32),
            per_head, folded, folded, pltpu.VMEM((nodes, 256), BF16), folded, folded,
            pick, pick, blocks, blocks, blocks, blocks, turned, turned,
            pltpu.VMEM((BLK, nodes), F32),
            pltpu.VMEM((2, listed * BLK, 256), F32), pltpu.VMEM((1, nodes), F32),
            pltpu.VMEM((nblk // 4, listed * BLK, 256), BF16),
            pltpu.VMEM((BLK, nodes), BF16),
            pltpu.VMEM((nodes, 128), BF16),
            pltpu.VMEM((nblk * listed + 1, BLK, 128), BF16),
            pltpu.VMEM((nodes, 256), BF16),
            folded, per_head, folded, folded, per_head, folded,
            big,
            pltpu.VMEM((SIDE, share, depth), F32),
            half, half, pltpu.VMEM((SIDE, SIDE, share // 2, depth), F32), half,
            pltpu.VMEM((2, side, SIDE, rows, depth), BF16),
            pltpu.VMEM((2, SIDE, rows, depth), BF16),
            pltpu.VMEM((2, side, rows, depth), BF16),
            pltpu.VMEM((nz, share // 2, depth // nz), BF16),
            pltpu.VMEM((few, share // 2, depth // nz), BF16),
            pltpu.VMEM((2, nz, share // 2, depth // nz), BF16),
            pltpu.SemaphoreType.DMA((5,)), pltpu.SemaphoreType.DMA((5,)), pltpu.SemaphoreType.DMA,
            dma(2, side), dma(2, side), dma(4, side), dma(seq - 1), dma(seq - 1), dma(seq - 1),
            dma(seq - 1), dma(seq - 1), dma(seq - 1), dma(SIDE), dma(SIDE + 1, side), dma(2, side),
            dma(few), dma(nz),
        ],
        compiler_params=pltpu.CompilerParams(
            collective_id=0, has_side_effects=True, vmem_limit_bytes=62 * 1024 * 1024),
        name="layer",
    )(cols, count, cols, count.reshape(1, nblk), order.reshape(nodes // 128, 128), q, k, v, g, wt)


def finish_kernel(*refs):
    arrays, outs, held, (load_sem, store_sem) = refs[:5], refs[5:10], refs[10:15], refs[15:]
    loads = [
        pltpu.make_async_copy(src, dst, load_sem.at[i])
        for i, (src, dst) in enumerate(zip(arrays, held))]
    stores = [
        pltpu.make_async_copy(src, dst, store_sem.at[i])
        for i, (src, dst) in enumerate(zip(held, outs))]
    for load in loads:
        load.start()
    for load, store in zip(loads, stores):
        load.wait()
        store.start()
    for store in stores:
        store.wait()


def finish(arrays):
    hbm = pl.BlockSpec(memory_space=pl.ANY)
    return pl.pallas_call(
        finish_kernel,
        out_shape=tuple(jax.ShapeDtypeStruct(a.shape, a.dtype) for a in arrays),
        in_specs=[hbm] * 5,
        out_specs=(hbm,) * 5,
        scratch_shapes=[pltpu.VMEM(a.shape, a.dtype) for a in arrays]
        + [pltpu.SemaphoreType.DMA((5,)), pltpu.SemaphoreType.DMA((5,))],
        compiler_params=pltpu.CompilerParams(vmem_limit_bytes=62 * 1024 * 1024),
        name="finish",
    )(*arrays)


def on_device(queries, key_vectors, value_vectors, out_grad, proj_weight,
              cluster_order, block_cols, block_count):
    seq, dps = lax.axis_size("seq"), lax.axis_size("dp")
    layer, dq, dk, dv, wg = finish(fused(
        queries[0], key_vectors[0], value_vectors[0], out_grad[0], proj_weight.T,
        cluster_order[0], block_cols[0].T, block_count[0], seq, dps))
    return layer[None], dq[None], dk[None], dv[None], wg.T


def solution(mesh):
    rows = P("dp", "seq", None)
    return jax.shard_map(
        on_device,
        mesh=mesh,
        in_specs=(rows, rows, rows, rows, P(None, "seq"),
                  P("dp", None), P("dp", None, None), P("dp", None)),
        out_specs=(rows, rows, rows, rows, P(None, "seq")),
        check_vma=False,
    )
```
